32 devices in a mesh: row: 4 (over z), col: 8 (over y, x, core).
Axes of the slice: x: 2, y: 2, z: 4, core: 2. Of those that a mesh axis runs over, the one named last changes fastest.
Arguments:
- offsets: float32 [4, 8, 2, 256], P('row', 'col'), may hold values from 0 to 1
- point_order: int32 [4, 8, 256], P('row', 'col'), may hold values from 0 to 255, each once within a row
- nugget: float32 [4, 8, 256], P('row', 'col'), may hold values from 1 to 4
- interp: float32 [4, 8, 128, 128], P('row', 'col'), may hold values from -0.5 to 0.5
Outputs:
- root_work: float32 [4096, 4096], P('row', 'col')
The draws below stay inside these ranges and needn't reach their ends.
Inputs may be any that keep to these rules, and one draw needn't show every extreme that they name: `point_order`: each row lists every point of its box once; its first 128 entries name the box's skeleton points.
All inputs are finite; a program needn't handle non-finite values.
Results may differ from the reference program's by a relative error of at most 0.0001.
Values sent between devices are 32-bit elements; how exact they have to be, the bound alone decides.
No kernel may reach another device: no remote copies, remote signals or barrier semaphores. Data moves between devices by JAX's collectives and lax.ppermute only.
A program may use at most 128 MiB of HBM per device.

```python
import math
import jax
import jax.numpy as jnp
from jax import lax

PTS = 256
SK = 128
PW = 512
RD = 128
BOX_ROWS = 4
BOX_COLS = 8
BOXES = 32
NR = 4096
N_ROW = 4
N_COL = 8


def level_of(rng, dims, split, smallest, largest):
    loudness = 1.0
    for position, shards_of in split:
        steps = jax.random.uniform(jax.random.fold_in(jax.random.fold_in(rng, 6), position), (shards_of,), jnp.float32, smallest / len(split), largest / len(split))
        loudness = loudness * jnp.repeat(jnp.exp(steps), dims[position] // shards_of).reshape((-1,) + (1,) * (len(dims) - 1 - position))
    return loudness


def bell_draw(rng, dims, scale, bound, cuts=(), held_as=jnp.bfloat16):
    entries = scale * jax.random.normal(rng, dims, jnp.float32)
    if cuts:
        entries = entries * level_of(rng, dims, cuts, -0.22, 0.18)
    return jnp.clip(entries, -bound, bound).astype(held_as)


def setup_inputs(seed: int = 0) -> dict:
    arg_keys = jax.random.split(jax.random.key(seed), 5)
    return {
        "offsets": jnp.clip(1.0 * jax.random.uniform(arg_keys[0], (BOX_ROWS, BOX_COLS, 2, PTS), jnp.float32) ** level_of(arg_keys[0], (BOX_ROWS, BOX_COLS, 2, PTS), ((0, 4), (1, 8)), -0.2, 0.2), 0.0, 1.0),
        "point_order": jax.vmap(lambda own: jax.random.permutation(own, PTS))(jax.random.split(arg_keys[1], BOX_ROWS * BOX_COLS)).reshape((BOX_ROWS, BOX_COLS, PTS)).astype(jnp.int32),
        "nugget": jnp.clip(jnp.exp(math.log(4.0) - 1.3862944 * jax.random.uniform(arg_keys[2], (BOX_ROWS, BOX_COLS, PTS), jnp.float32) ** level_of(arg_keys[2], (BOX_ROWS, BOX_COLS, PTS), ((0, 4), (1, 8)), -0.2, 0.2)), 1.0, 4.0),
        "interp": bell_draw(arg_keys[3], (BOX_ROWS, BOX_COLS, SK, RD), SK ** -0.5, 0.5, ((0, 4), (1, 8)), jnp.float32),
    }


kernel_amp = 0.015625
kernel_len = 0.5
highest = lax.Precision.HIGHEST

def offsets_all():
    return [(a, b) for a in (-1, 0, 1) for b in (-1, 0, 1)]

def block_of(a, b):
    return (a + 1) * 3 + (b + 1)

def kernel(left, right):
    gap_row = left[..., 0, :, None] - right[..., 0, None, :]
    gap_col = left[..., 1, :, None] - right[..., 1, None, :]
    return kernel_amp * jnp.exp(-jnp.sqrt(gap_row * gap_row + gap_col * gap_col) / kernel_len)

def shifted(padded, start_row, start_col, step):
    count_rows = N_ROW // step
    count_cols = N_COL // step
    return padded[start_row:start_row + step * (count_rows - 1) + 1:step, start_col:start_col + step * (count_cols - 1) + 1:step]

def cross_sum(neighbours, target, columns):
    left_rows = []
    right_rows = []
    for e in offsets_all():
        if abs(target[0] - e[0]) <= 1 and abs(target[1] - e[1]) <= 1:
            source = neighbours[block_of(e[0], e[1])]
            home_slot = block_of(-e[0], -e[1])
            other_slot = block_of(target[0] - e[0], target[1] - e[1])
            left_rows.append(source[..., home_slot * PTS:home_slot * PTS + columns])
            right_rows.append(source[..., other_slot * PTS:other_slot * PTS + columns])
    return jnp.einsum('uvrk,uvrl->uvkl', jnp.concatenate(left_rows, axis=-2), jnp.concatenate(right_rows, axis=-2), precision=highest)

def reference(offsets, point_order, nugget, interp):
    row_pos = jnp.broadcast_to(jnp.arange(N_ROW, dtype=jnp.float32)[:, None], (N_ROW, N_COL))
    col_pos = jnp.broadcast_to(jnp.arange(N_COL, dtype=jnp.float32)[None, :], (N_ROW, N_COL))
    corner = jnp.stack([row_pos, col_pos], axis=2)[..., None]
    points = jnp.take_along_axis(offsets + corner, jnp.broadcast_to(point_order[:, :, None, :], offsets.shape), axis=3)
    weights = jnp.take_along_axis(nugget, point_order, axis=2)
    padded_points = jnp.pad(points, ((1, 1), (1, 1), (0, 0), (0, 0)))
    present = jnp.pad(jnp.ones((N_ROW, N_COL), jnp.float32), 1)
    factors = jnp.zeros((N_ROW, N_COL, RD, 9 * PTS), jnp.float32)
    for a in (0, 1):
        for b in (0, 1):
            own_points = shifted(points, a, b, 2)
            weights_sub = shifted(weights, a, b, 2)
            interp_sub = shifted(interp, a, b, 2)
            padded_factors = jnp.pad(factors, ((1, 1), (1, 1), (0, 0), (0, 0)))
            neighbours = [shifted(padded_factors, 1 + a + c, 1 + b + d, 2) for c, d in offsets_all()]
            kernel_blocks = []
            for c, d in offsets_all():
                present_box = shifted(present, 1 + a + c, 1 + b + d, 2)[..., None, None]
                kernel_block = kernel(own_points, shifted(padded_points, 1 + a + c, 1 + b + d, 2)) * present_box
                if (c, d) == (0, 0):
                    kernel_block = kernel_block + weights_sub[..., :, None] * jnp.eye(PTS, dtype=jnp.float32)
                kernel_blocks.append(kernel_block)
            near_matrix = jnp.concatenate(kernel_blocks, axis=-1)
            fill_blocks = [cross_sum(neighbours, m, PTS) for m in offsets_all()]
            matrix = near_matrix - jnp.concatenate(fill_blocks, axis=-1)
            reduced_rows = matrix[..., SK:, :] - jnp.einsum('uvsr,uvsk->uvrk', interp_sub, matrix[..., :SK, :], precision=highest)
            centre = reduced_rows[..., 4 * PTS:5 * PTS]
            reduced = centre[..., SK:] - jnp.einsum('uvrs,uvst->uvrt', centre[..., :SK], interp_sub, precision=highest)
            diag_factor = jnp.linalg.cholesky(reduced)
            solved = jax.scipy.linalg.solve_triangular(diag_factor, reduced_rows, lower=True)
            factors = factors.at[a::2, b::2].set(solved)
    padded_factors = jnp.pad(factors, ((1, 1), (1, 1), (0, 0), (0, 0)))
    neighbours = [shifted(padded_factors, 1 + c, 1 + d, 1) for c, d in offsets_all()]
    deltas = []
    for c, d in offsets_all():
        fill_part = cross_sum(neighbours, (c, d), SK)
        present_box = shifted(present, 1 + c, 1 + d, 1)[..., None, None]
        if (c, d) == (0, 0):
            delta_block = weights[..., :SK, None] * jnp.eye(SK, dtype=jnp.float32) - fill_part
        else:
            delta_block = -fill_part
        deltas.append(delta_block * present_box)
    deltas = jnp.stack(deltas, axis=2)
    skeleton = points[..., :SK].reshape(BOXES, 2, SK)
    all_skeleton = jnp.transpose(skeleton, (1, 2, 0)).reshape(2, NR)
    row_blocks = jnp.transpose(skeleton, (2, 1, 0))
    root_matrix = lax.map(lambda row_block: kernel(row_block, all_skeleton), row_blocks).reshape(NR, NR)
    box_row = jnp.arange(N_ROW, dtype=jnp.int32)[:, None]
    box_col = jnp.arange(N_COL, dtype=jnp.int32)[None, :]
    sources = []
    targets = []
    for c, d in offsets_all():
        inside = (box_row + c >= 0) & (box_row + c < N_ROW) & (box_col + d >= 0) & (box_col + d < N_COL)
        home_box = box_row * N_COL + box_col
        sources.append(home_box)
        targets.append(jnp.where(inside, (box_row + c) * N_COL + box_col + d, home_box).astype(jnp.int32))
    sources = jnp.stack(sources, axis=2).astype(jnp.int32)
    targets = jnp.stack(targets, axis=2).astype(jnp.int32)
    blocks = root_matrix.reshape(SK, BOXES, SK, BOXES).at[:, sources, :, targets].add(deltas)
    root_matrix = blocks.reshape(NR, NR)
    rows_all = jnp.arange(NR, dtype=jnp.int32)[:, None]
    panels = []
    for p in range(2):
        first_col = p * PW
        diag_factor = jnp.linalg.cholesky(root_matrix[first_col:first_col + PW, first_col:first_col + PW])
        solved = jax.scipy.linalg.solve_triangular(diag_factor, root_matrix[:, first_col:first_col + PW].T, lower=True).T
        column = jnp.where(rows_all < first_col, 0.0, solved.at[first_col:first_col + PW].set(diag_factor))
        root_matrix = root_matrix - jnp.dot(column, column.T, precision=highest)
        panels.append(column)
    root_matrix = root_matrix.at[:, :PW].set(panels[0]).at[:, PW:2 * PW].set(panels[1]).at[:2 * PW, 2 * PW:].set(0.0)
    return root_matrix
```

```python
import functools

import jax
import jax.numpy as jnp
from jax import lax
from jax.experimental import pallas as pl
from jax.experimental.pallas import tpu as pltpu
from jax.sharding import PartitionSpec as P

PW = 512
PANELS = 2
kernel_amp = 0.015625
kernel_len = 0.5
f32 = jnp.float32
bf16 = jnp.bfloat16
BLK = 128
SUB = 16
TILE = 256
VMEM = pltpu.CompilerParams(vmem_limit_bytes=56 * 1024 * 1024)
OFFS = [(a, b) for a in (-1, 0, 1) for b in (-1, 0, 1)]


def idx(a, b):
    return (a + 1) * 3 + (b + 1)


def split(x):
    hi = x.astype(bf16)
    return hi, (x - hi.astype(f32)).astype(bf16)


def dot(a, b, nt=False):
    dims = ((1,), (1,)) if nt else ((1,), (0,))
    return lax.dot_general(a, b, (dims, ((), ())), preferred_element_type=f32)


def dot_pair(a, b, nt=False):
    return dot(a[0], b[0], nt) + (dot(a[0], b[1], nt) + dot(a[1], b[0], nt))


def dot3(a, b):
    return dot_pair(split(a), split(b))


def kap(cx, cy, rx, ry, amp):
    dx = cx - rx
    dy = cy - ry
    d2 = dx * dx + dy * dy
    dist = d2 * lax.rsqrt(jnp.maximum(d2, 1e-30))
    return amp * jnp.exp(dist * (-1.0 / kernel_len))


def column_of(row):
    return jnp.broadcast_to(row, (BLK, BLK)).T


def eye(n):
    return lax.broadcasted_iota(jnp.int32, (n, n), 0) == lax.broadcasted_iota(
        jnp.int32, (n, n), 1
    )


def factor(mats):
    n = mats[0].shape[0]
    w = SUB
    unit = eye(n).astype(f32)
    cur = [jnp.concatenate([m, unit], axis=1) for m in mats]
    out = [[] for _ in mats]
    rows = lax.broadcasted_iota(jnp.int32, (w, 1), 0)
    many = range(len(mats))

    def wide(x):
        return jnp.concatenate([x, x], axis=1)

    for p in range(n // w):
        lo = p * w
        fwd = [c[:w] for c in cur]
        full = list(fwd)
        col = [[jnp.broadcast_to(f[:, lo + t : lo + t + 1], (w, n)) for t in range(w)] for f in fwd]
        for t in range(w):
            for q in many:
                r = lax.rsqrt(col[q][t][t : t + 1])
                out[q].append(fwd[q][t : t + 1] * wide(r))
                rp = r * r
                scaled = col[q][t] * rp
                fwd_new = fwd[q] - wide(scaled) * fwd[q][t : t + 1]
                g = full[q][t : t + 1] * wide(rp)
                full[q] = jnp.where(rows == t, g, full[q] - wide(col[q][t]) * g)
                for v in range(t + 1, w):
                    c = col[q][v]
                    col[q][v] = jnp.where(rows == t, c * rp, c - scaled * c[t : t + 1])
                fwd[q] = fwd_new
        rest = n - lo - w
        if rest > 0:
            for q in many:
                parts = [full[q], jnp.zeros((rest, 2 * n), f32)]
                if lo > 0:
                    parts = [jnp.zeros((lo, 2 * n), f32)] + parts
                below = cur[q][w:]
                cur[q] = below - dot3(below[:, :n], jnp.concatenate(parts, axis=0))
    return [jnp.concatenate(o, axis=0) for o in out]


class Boxes:
    def __init__(self, sides):
        self.sides = sides
        self.kept = {}

    def row(self, c, n):
        return self.sides[c[1]][c[0] + 1, BLK + n : BLK + n + 1, :]

    def once(self, key, make):
        if key not in self.kept:
            self.kept[key] = make()
        return self.kept[key]

    def interp(self, c):
        return self.once(("i", c), lambda: split(self.sides[c[1]][c[0] + 1, :BLK, :]))

    def interp_t(self, c):
        return self.once(("t", c), lambda: split(self.sides[c[1]][c[0] + 1, :BLK, :].T))

    def col(self, c, n):
        return self.once(("c", c, n), lambda: column_of(self.row(c, n)))

    def kernel(self, c, part, m, part_m):
        amp = kernel_amp * self.row(c, 6) * self.row(m, 6)
        value = kap(
            self.col(c, part),
            self.col(c, 2 + part),
            self.row(m, part_m),
            self.row(m, 2 + part_m),
            amp,
        )
        if c == m and part == part_m:
            weight = self.row(c, 4 + part) + (1.0 - self.row(c, 6))
            value = value + jnp.where(eye(BLK), weight, 0.0)
        return value

    def rows_of(self, c, wanted):
        result = {}
        wanted = list(wanted)
        for n in range(0, len(wanted), 2):
            pair = wanted[n : n + 2]
            skel = jnp.concatenate([self.kernel(c, 0, m, p) for m, p in pair], axis=1)
            red = jnp.concatenate([self.kernel(c, 1, m, p) for m, p in pair], axis=1)
            value = red - dot_pair(self.interp_t(c), split(skel))
            for k, key in enumerate(pair):
                result[key] = value[:, k * BLK : (k + 1) * BLK]
        return result


def reduced(pair, interp):
    return pair[1] - dot_pair(split(pair[0]), interp)


def subtract_fill(rows, factor_e, at, interp, keys):
    gain = split(reduced((factor_e[at, 0], factor_e[at, 1]), interp).T)
    keys = [k for k in keys if k in rows]
    for n in range(0, len(keys), 2):
        pair = keys[n : n + 2]
        value = dot_pair(gain, split(jnp.concatenate([factor_e[k] for k in pair], axis=1)))
        for k, key in enumerate(pair):
            rows[key] = rows[key] - value[:, k * BLK : (k + 1) * BLK]


def solve(rows_list, centres, interps):
    mats = [reduced((r[c, 0], r[c, 1]), i) for r, c, i in zip(rows_list, centres, interps)]
    inverses = [split(u[:, BLK:]) for u in factor(mats)]
    results = []
    for rows, centre, inv in zip(rows_list, centres, inverses):
        keys = [k for k in rows if k != (centre, 1)]
        result = {}
        for n in range(0, len(keys), 2):
            pair = keys[n : n + 2]
            value = dot_pair(inv, split(jnp.concatenate([rows[k] for k in pair], axis=1)))
            for k, key in enumerate(pair):
                result[key] = value[:, k * BLK : (k + 1) * BLK]
        results.append(result)
    return results


def zero_fill(ref, start=0):
    for n in range(start, ref.shape[0]):
        ref[n] = jnp.zeros(ref.shape[1:], f32)


OWN = (0, 0)
ALL_SKEL = [(m, 0) for m in OFFS]


def first_kernel(colour, mid, left, right, h_ref, f_ref, to_left, to_right):
    boxes = Boxes({0: mid, -1: left, 1: right})
    if colour < 2:
        zero_fill(h_ref)
        zero_fill(to_left)
        zero_fill(to_right)
    else:
        zero_fill(f_ref)
    own_keys = ALL_SKEL + [(OWN, 1)]
    if colour == 0:
        sources = []
        wanted = []
    elif colour == 1:
        sources = [(0, b) for b in (-1, 1)]
        wanted = [
            [(OWN, 0), (OWN, 1), ((-1, 0), 0), ((1, 0), 0)]
            + [((a, b), 0) for a in (-1, 0, 1)]
            + [((0, b), 1)]
            for _, b in sources
        ]
    elif colour == 2:
        sources = [(a, 0) for a in (-1, 1)]
        wanted = [
            [((0, b), p) for b in (-1, 0, 1) for p in (0, 1)]
            + [((a, b), 0) for b in (-1, 0, 1)]
            + [((a, 0), 1)]
            for a, _ in sources
        ]
        own_keys = own_keys + [((0, -1), 1), ((0, 1), 1)]
    else:
        sources = [(a, b) for a in (-1, 1) for b in (-1, 1)]
        wanted = [
            [(m, p) for m in (OWN, (a, 0), (0, b), (a, b)) for p in (0, 1)] for a, b in sources
        ]
    if sources:
        first = solve(
            [boxes.rows_of(c, k) for c, k in zip(sources, wanted)],
            sources,
            [boxes.interp(c) for c in sources],
        )
        first = dict(zip(sources, first))
    own = boxes.rows_of(OWN, own_keys)
    for e in sources:
        subtract_fill(own, first[e], OWN, boxes.interp(OWN), first[e].keys())
    if colour < 2:
        result = solve([own], [OWN], [boxes.interp(OWN)])[0]
        for m in OFFS:
            f_ref[idx(*m)] = result[m, 0]
        return
    if colour == 3:
        second_at = [(-1, 0), (1, 0)]
        rows = []
        for a, _ in second_at:
            keys = [((a, 0), 0), ((a, 0), 1), (OWN, 0), (OWN, 1)]
            keys += [((0, b), p) for b in (-1, 1) for p in (0, 1)]
            keys += [((a, b), 0) for b in (-1, 1)]
            part = boxes.rows_of((a, 0), keys)
            for b in (-1, 1):
                f = first[a, b]
                subtract_fill(part, f, (a, 0), boxes.interp((a, 0)), f.keys())
            rows.append(part)
        second = solve(rows, second_at, [boxes.interp(c) for c in second_at])
        for c, f in zip(second_at, second):
            subtract_fill(own, f, OWN, boxes.interp(OWN), f.keys())
        for b, ref in ((-1, to_left), (1, to_right)):
            total = {}
            at = (0, b)
            order = [((a, v), 0) for a in (-1, 0, 1) for v in (b, 0)] + [(at, 1), (OWN, 1)]
            for key in order:
                total[key] = jnp.zeros((BLK, BLK), f32)
            for f in second:
                subtract_fill(total, f, at, boxes.interp(at), f.keys())
            for n, key in enumerate(order):
                ref[n] = -total[key]
    for key, value in own.items():
        if key[1] == 0:
            h_ref[idx(*key[0])] = value
        else:
            h_ref[red_slot(key[0][1])] = value


def red_slot(b):
    return {0: 9, -1: 10, 1: 11}[b]


def second_kernel(h_ref, from_left, from_right, interp, f_ref, to_left, to_right):
    rows = {(m, 0): h_ref[idx(*m)] for m in OFFS}
    for b in (-1, 0, 1):
        rows[(0, b), 1] = h_ref[red_slot(b)]
    for b, ref in ((-1, from_left), (1, from_right)):
        order = [((a, v), 0) for a in (-1, 0, 1) for v in (0, b)] + [(OWN, 1), ((0, b), 1)]
        for n, key in enumerate(order):
            rows[key] = rows[key] - ref[n]
    result = solve([rows], [OWN], [split(interp[...])])[0]
    for m in OFFS:
        f_ref[idx(*m)] = result[m, 0]
    for b, ref in ((-1, to_left), (1, to_right)):
        for n, key in enumerate(
            [((a, v), 0) for a in (-1, 0, 1) for v in (0, b)] + [((0, b), 1)]
        ):
            ref[n] = result[key]


def side_blocks(values, to_left, to_right):
    for b, ref in ((-1, to_left), (1, to_right)):
        for n, m in enumerate([(a, v) for a in (-1, 0, 1) for v in (0, b)]):
            ref[n] = values[m]


def third_kernel(h_ref, from_left, from_right, interp, f_ref, to_left, to_right):
    rows = {(m, 0): h_ref[idx(*m)] for m in OFFS}
    rows[OWN, 1] = h_ref[9]
    own_interp = split(interp[...])
    for b, ref in ((-1, from_left), (1, from_right)):
        f = {}
        for n, key in enumerate(
            [((a, v), 0) for a in (-1, 0, 1) for v in (b, 0)] + [(OWN, 1)]
        ):
            f[key] = ref[n]
        subtract_fill(rows, f, OWN, own_interp, f.keys())
    result = solve([rows], [OWN], [own_interp])[0]
    values = {m: result[m, 0] for m in OFFS}
    for m in OFFS:
        f_ref[idx(*m)] = values[m]
    side_blocks(values, to_left, to_right)


def pass_kernel(old_ref, f_ref, to_left, to_right):
    values = {m: old_ref[idx(*m)] for m in OFFS}
    for m in OFFS:
        f_ref[idx(*m)] = values[m]
    side_blocks(values, to_left, to_right)


def sums_kernel(f_ref, from_left, from_right, t_ref, up_ref, down_ref):
    f = {OWN: {m: split(f_ref[idx(*m)]) for m in OFFS}}
    for b, ref in ((-1, from_left), (1, from_right)):
        f[0, b] = {
            m: split(ref[n]) for n, m in enumerate([(a, v) for a in (-1, 0, 1) for v in (b, 0)])
        }
    turned = {
        (e, a): tuple(x.T for x in split_f32(f_ref, from_left, from_right, e, a))
        for e in f
        for a in (-1, 0, 1)
    }
    for a, ref in ((-1, up_ref), (0, t_ref), (1, down_ref)):
        across = [m for m in OFFS if a == 0 or m[0] in (0, a)]
        for n, m in enumerate(across):
            total = None
            for e in f:
                if m in f[e]:
                    term = dot_pair(split(turned[e, a][0]), f[e][m])
                    total = term if total is None else total + term
            ref[n] = total


def split_f32(f_ref, from_left, from_right, e, a):
    if e == OWN:
        return (f_ref[idx(a, 0)],)
    ref = from_left if e[1] < 0 else from_right
    return (ref[2 * (a + 1) + 1],)


def assemble(pack_ref, row_ref, col_ref, out_ref, colx, coly, grid_cols):
    boxes, height, _ = pack_ref.shape
    width = out_ref.shape[1]
    per = TILE // boxes
    depth = 9 * per
    tiles = width // TILE
    for i in range(out_ref.shape[0] // BLK):
        colx[i * BLK : (i + 1) * BLK, :] = column_of(row_ref[0:1, i * BLK : (i + 1) * BLK])
        coly[i * BLK : (i + 1) * BLK, :] = column_of(row_ref[1:2, i * BLK : (i + 1) * BLK])
    r = lax.broadcasted_iota(jnp.int32, (depth, TILE), 0)
    c = lax.broadcasted_iota(jnp.int32, (depth, TILE), 1)
    n, inner = r // per, r % per
    box = c % boxes
    same = inner == c // boxes
    box_row, box_col = box // grid_cols - (n // 3 - 1), box % grid_cols - (n % 3 - 1)

    def group(g, carry):
        values = []
        for s in range(8):
            b = g * 8 + s
            hot = same & (box_row == b // grid_cols) & (box_col == b % grid_cols)
            hot = hot.astype(f32).astype(bf16)
            data = pack_ref[b]
            data = jnp.concatenate(
                [data[:, t * depth : (t + 1) * depth] for t in range(tiles)], axis=0
            )
            hi, lo = split(data)
            values.append(dot(hi, hot) + dot(lo, hot))
        for t in range(tiles):
            part = jnp.stack([v[t * height : (t + 1) * height] for v in values], axis=0)
            part = jnp.swapaxes(part, 0, 1)
            rx = col_ref[0:1, t * TILE : (t + 1) * TILE]
            ry = col_ref[1:2, t * TILE : (t + 1) * TILE]
            for k in range(height):
                at = pl.ds(pl.multiple_of(k * boxes + g * 8, 8), 8)
                cx, cy = colx[at, :], coly[at, :]
                cx = jnp.concatenate([cx, cx], axis=1)
                cy = jnp.concatenate([cy, cy], axis=1)
                out_ref[at, t * TILE : (t + 1) * TILE] = part[k] + kap(cx, cy, rx, ry, kernel_amp)
        return carry

    lax.fori_loop(0, boxes // 8, group, 0)


def lead_kernel(grid_cols, pack_ref, pts_ref, uh_ref, ul_ref, ih_ref, il_ref, mat, colx, coly, rh, rl):
    assemble(pack_ref, pts_ref, pts_ref, mat, colx, coly, grid_cols)
    size = mat.shape[0]
    count = size // BLK

    def step(p, carry):
        at = pl.ds(pl.multiple_of(p * BLK, BLK), BLK)
        inv = factor([mat[at, at]])[0][:, BLK:]
        mine = dot_pair(split(inv), split(mat[at, :]))
        mat[at, :] = mine
        hi, lo = split(mine)
        rh[...] = hi
        rl[...] = lo
        uh_ref[at, :] = hi
        ul_ref[at, :] = lo
        turned = inv.T
        half = p % 2
        th, tl = split(turned)

        @pl.when(half == 0)
        def _():
            ih_ref[at, :BLK] = th
            il_ref[at, :BLK] = tl

        @pl.when(half == 1)
        def _():
            before = pl.ds(pl.multiple_of((p - 1) * BLK, BLK), BLK)
            first = ih_ref[before, :BLK], il_ref[before, :BLK]
            between = split(mat[before, at])
            corner = -dot_pair(split(dot_pair(first, between)), (th, tl))
            ch, cl = split(corner)
            ih_ref[before, BLK:] = ch
            il_ref[before, BLK:] = cl
            ih_ref[at, :BLK] = jnp.zeros((BLK, BLK), bf16)
            il_ref[at, :BLK] = jnp.zeros((BLK, BLK), bf16)
            ih_ref[at, BLK:] = th
            il_ref[at, BLK:] = tl

        def update(j, carry):
            there = pl.ds(pl.multiple_of(j * BLK, BLK), BLK)
            left = split(mat[at, there].T)
            mat[there, :] = mat[there, :] - dot_pair(left, (rh[...], rl[...]))
            return carry

        lax.fori_loop(p + 1, count, update, 0)
        return carry

    lax.fori_loop(0, count, step, 0)


def tile_kernel(
    grid_cols,
    place,
    xy_pack,
    own_pack,
    xy_pts,
    lead_pts,
    row_pts,
    col_pts,
    uh_ref,
    ul_ref,
    ih_ref,
    il_ref,
    out_ref,
    mat,
    colx,
    coly,
    ph,
    plo,
):
    assemble(xy_pack, xy_pts, lead_pts, mat, colx, coly, grid_cols)
    total, size = mat.shape
    rows, cols = out_ref.shape
    pair = 2 * BLK
    chunk = 256

    def solve_rows(c, carry):
        at = pl.ds(pl.multiple_of(c * chunk, chunk), chunk)
        for p in range(size // pair):
            here = slice(p * pair, (p + 1) * pair)
            acc = mat[at, here]
            if p > 0:
                before = slice(0, p * pair)
                acc = acc - dot_pair(
                    (ph[at, before], plo[at, before]), (uh_ref[before, here], ul_ref[before, here])
                )
            value = dot_pair(split(acc), (ih_ref[here, :], il_ref[here, :]))
            mat[at, here] = value
            hi, lo = split(value)
            ph[at, here] = hi
            plo[at, here] = lo
        return carry

    lax.fori_loop(0, total // chunk, solve_rows, 0)
    first_row, first_col = place[0], place[1]

    @pl.when(first_col < size)
    def _():
        r = first_row + lax.broadcasted_iota(jnp.int32, (rows, cols), 0)
        c = first_col + lax.broadcasted_iota(jnp.int32, (rows, cols), 1)
        start = pl.multiple_of(first_col, BLK)
        out_ref[...] = jnp.where(r >= c, mat[:rows, pl.ds(start, cols)], 0.0)

    @pl.when(first_col >= size)
    def _():
        assemble(own_pack, row_pts, col_pts, out_ref, colx, coly, grid_cols)

        def update(c, carry):
            at = pl.ds(pl.multiple_of(c * chunk, chunk), chunk)
            value = out_ref[at, :] - dot_pair(
                (ph[at, :], plo[at, :]), (ph[rows:, :], plo[rows:, :]), nt=True
            )
            r = first_row + c * chunk + lax.broadcasted_iota(jnp.int32, (chunk, cols), 0)
            out_ref[at, :] = jnp.where(r >= size, value, 0.0)
            return carry

        lax.fori_loop(0, rows // chunk, update, 0)


def blocks(*counts):
    return [jax.ShapeDtypeStruct((n, BLK, BLK), f32) for n in counts]


def on_device(offsets, point_order, nugget, interp):
    row_at = lax.axis_index("row")
    col_at = lax.axis_index("col")
    row_count = lax.axis_size("row")
    col_count = lax.axis_size("col")
    box_total = row_count * col_count
    skel = interp.shape[2]
    box_id = row_at * col_count + col_at
    both = ("row", "col")

    corner = jnp.stack([row_at, col_at]).astype(f32)[:, None]
    table = jnp.concatenate([offsets[0, 0] + corner, nugget[0, 0][None]], axis=0)
    table = jnp.take(table, point_order[0, 0], axis=1)
    details = jnp.concatenate(
        [table.reshape(6, BLK), jnp.ones((1, BLK), f32), jnp.zeros((1, BLK), f32)], axis=0
    )
    packed = jnp.concatenate([interp[0, 0], details], axis=0)
    skeleton = jnp.concatenate([table[:2, :skel], jnp.zeros((6, skel), f32)], axis=0)
    everyone = lax.all_to_all(
        jnp.broadcast_to(skeleton[None], (box_total,) + skeleton.shape),
        both,
        split_axis=0,
        concat_axis=0,
        tiled=True,
    )

    def hop(x, axis, distance):
        count = lax.axis_size(axis)
        return lax.ppermute(
            x, axis, [(i, i + distance) for i in range(count) if 0 <= i + distance < count]
        )

    def side_hop(x, distance, row_odd, col_odd):
        pairs = [
            (i * col_count + j, i * col_count + j + distance)
            for i in range(row_count)
            for j in range(col_count)
            if i % 2 == row_odd and j % 2 == col_odd and 0 <= j + distance < col_count
        ]
        return lax.ppermute(x, both, pairs)

    mid = jnp.stack([hop(packed, "row", 1), packed, hop(packed, "row", -1)])
    left = hop(mid, "col", 1)
    right = hop(mid, "col", -1)
    colour = 2 * (row_at % 2) + col_at % 2

    def first(n):
        def run(a, b, c):
            return pl.pallas_call(
                functools.partial(first_kernel, n),
                out_shape=blocks(12, 9, 8, 8),
                compiler_params=VMEM,
                name=f"first_{n}",
            )(a, b, c)

        return run

    h_rows, f_own, pay_left, pay_right = lax.switch(
        colour, [first(n) for n in range(4)], mid, left, right
    )
    from_right = side_hop(pay_left, -1, 1, 1)
    from_left = side_hop(pay_right, 1, 1, 1)
    own_interp = interp[0, 0]
    f_own, pay_left, pay_right = lax.cond(
        colour == 2,
        lambda f, *a: tuple(
            pl.pallas_call(
                second_kernel, out_shape=blocks(9, 7, 7), compiler_params=VMEM, name="second"
            )(*a)
        ),
        lambda f, *a: (f,) + tuple(jnp.zeros((7, BLK, BLK), f32) for _ in range(2)),
        f_own,
        h_rows,
        from_left,
        from_right,
        own_interp,
    )
    from_right = side_hop(pay_left, -1, 1, 0)
    from_left = side_hop(pay_right, 1, 1, 0)
    f_own, pay_left, pay_right = lax.cond(
        colour == 3,
        lambda f, *a: tuple(
            pl.pallas_call(
                third_kernel, out_shape=blocks(9, 6, 6), compiler_params=VMEM, name="third"
            )(*a)
        ),
        lambda f, *a: tuple(
            pl.pallas_call(
                pass_kernel, out_shape=blocks(9, 6, 6), compiler_params=VMEM, name="passed"
            )(f)
        ),
        f_own,
        h_rows,
        from_left,
        from_right,
        own_interp,
    )
    from_right = hop(pay_left, "col", -1)
    from_left = hop(pay_right, "col", 1)
    total, up, down = pl.pallas_call(
        sums_kernel, out_shape=blocks(9, 6, 6), compiler_params=VMEM, name="sums"
    )(f_own, from_left, from_right)
    from_below = hop(up, "row", -1)
    from_above = hop(down, "row", 1)
    delta = -(
        total
        + jnp.concatenate([jnp.zeros((3, BLK, BLK), f32), from_below], axis=0)
        + jnp.concatenate([from_above, jnp.zeros((3, BLK, BLK), f32)], axis=0)
    )
    centre = jnp.where(jnp.eye(skel, dtype=bool), table[2, :skel][None, :], 0.0)
    delta = delta.at[4].add(centre)

    lead = PANELS * PW
    lead_per = lead // box_total
    row_per = skel // row_count
    col_per = skel // col_count
    per = TILE // box_total

    def packed_rows(x):
        n, k, l = x.shape
        x = x.reshape(n, k, l // per, per)
        return jnp.transpose(x, (1, 2, 0, 3)).reshape(k, l // per * n * per)

    def exchange(x):
        return lax.all_to_all(x, both, split_axis=0, concat_axis=0, tiled=True)

    narrow = packed_rows(delta[:, :, :lead_per])
    lead_pack = exchange(
        jnp.broadcast_to(narrow[None, :lead_per], (box_total, lead_per, narrow.shape[1]))
    )
    row_parts = narrow.reshape(row_count, 1, row_per, -1)
    col_parts = narrow.reshape(1, col_count, col_per, -1)
    xy_pack = exchange(
        jnp.concatenate(
            [
                jnp.broadcast_to(row_parts, (row_count, col_count, row_per, narrow.shape[1])),
                jnp.broadcast_to(col_parts, (row_count, col_count, col_per, narrow.shape[1])),
            ],
            axis=2,
        ).reshape(box_total, row_per + col_per, -1)
    )
    whole = packed_rows(delta).reshape(row_count, row_per, col_count, -1)
    own_pack = exchange(jnp.transpose(whole, (0, 2, 1, 3)).reshape(box_total, row_per, -1))

    points = jnp.transpose(everyone[:, :2], (1, 2, 0))

    def flat(x):
        return jnp.pad(x.reshape(2, -1), ((0, 6), (0, 0)))

    lead_pts = flat(points[:, :lead_per])
    row_pts = lax.dynamic_slice_in_dim(points, row_at * row_per, row_per, 1)
    col_pts = lax.dynamic_slice_in_dim(points, col_at * col_per, col_per, 1)
    xy_pts = flat(jnp.concatenate([row_pts, col_pts], axis=1))
    row_pts, col_pts = flat(row_pts), flat(col_pts)
    rows_here = row_per * box_total
    cols_here = col_per * box_total
    upper_hi, upper_lo, inv_hi, inv_lo = pl.pallas_call(
        functools.partial(lead_kernel, col_count),
        out_shape=[jax.ShapeDtypeStruct((lead, lead), bf16)] * 2
        + [jax.ShapeDtypeStruct((lead, 2 * BLK), bf16)] * 2,
        scratch_shapes=[
            pltpu.VMEM((lead, lead), f32),
            pltpu.VMEM((lead, BLK), f32),
            pltpu.VMEM((lead, BLK), f32),
            pltpu.VMEM((BLK, lead), bf16),
            pltpu.VMEM((BLK, lead), bf16),
        ],
        compiler_params=VMEM,
        name="lead",
    )(lead_pack, lead_pts)
    place = jnp.stack([row_at * rows_here, col_at * cols_here]).astype(jnp.int32)
    vmem = pl.BlockSpec(memory_space=pltpu.VMEM)
    both_rows = rows_here + cols_here
    return pl.pallas_call(
        functools.partial(tile_kernel, col_count),
        in_specs=[pl.BlockSpec(memory_space=pltpu.SMEM)] + [vmem] * 10,
        out_specs=vmem,
        out_shape=jax.ShapeDtypeStruct((rows_here, cols_here), f32),
        scratch_shapes=[
            pltpu.VMEM((both_rows, lead), f32),
            pltpu.VMEM((both_rows, BLK), f32),
            pltpu.VMEM((both_rows, BLK), f32),
            pltpu.VMEM((both_rows, lead), bf16),
            pltpu.VMEM((both_rows, lead), bf16),
        ],
        compiler_params=VMEM,
        name="tile",
    )(
        place,
        xy_pack,
        own_pack,
        xy_pts,
        lead_pts,
        row_pts,
        col_pts,
        upper_hi,
        upper_lo,
        inv_hi,
        inv_lo,
    )


def solution(mesh):
    in_specs = (
        P("row", "col", None, None),
        P("row", "col", None),
        P("row", "col", None),
        P("row", "col", None, None),
    )
    return jax.shard_map(
        on_device, mesh=mesh, in_specs=in_specs, out_specs=P("row", "col"), check_vma=False
    )
```

```python
import functools
import math

import jax
import jax.numpy as jnp
from jax import lax
from jax.experimental import pallas as pl
from jax.experimental.pallas import tpu as pltpu
from jax.sharding import PartitionSpec as P

PW = 512
PANELS = 2
kernel_amp = 0.015625
kernel_len = 0.5
scale = math.log2(math.e) / kernel_len
log_amp = math.log2(kernel_amp)
f32 = jnp.float32
bf16 = jnp.bfloat16
BLK = 128
TILE = 256
VMEM = pltpu.CompilerParams(vmem_limit_bytes=56 * 1024 * 1024)
OFFS = [(a, b) for a in (-1, 0, 1) for b in (-1, 0, 1)]


def idx(a, b):
    return (a + 1) * 3 + (b + 1)


def split(x):
    hi = x.astype(bf16)
    return hi, (x - hi.astype(f32)).astype(bf16)


def dot(a, b, nt=False):
    dims = ((1,), (1,)) if nt else ((1,), (0,))
    return lax.dot_general(a, b, (dims, ((), ())), preferred_element_type=f32)


def dot_pair(a, b, nt=False):
    left = jnp.concatenate([a[0], a[1], a[0]], axis=1)
    return dot(left, jnp.concatenate([b[0], b[0], b[1]], axis=1 if nt else 0), nt)


def dot3(a, b):
    return dot_pair(split(a), split(b))


def kap(cx, cy, rx, ry):
    dx = cx - rx
    dy = cy - ry
    d2 = dx * dx + dy * dy
    dist = d2 * lax.rsqrt(jnp.maximum(d2, 1e-30))
    return jnp.exp2(log_amp - dist)


def column_of(row):
    return jnp.broadcast_to(row, (BLK, BLK)).T


def eye(n):
    return lax.broadcasted_iota(jnp.int32, (n, n), 0) == lax.broadcasted_iota(
        jnp.int32, (n, n), 1
    )


def factor(mats, beside=()):
    n = mats[0].shape[0]
    w, part = (32, 16) if len(mats) == 1 else (16, 8)
    steps = -(-len(beside) * w // n)
    groups = range(w // 8)
    many = range(len(mats))
    cur = list(mats)
    out = [[] for _ in mats]
    lane = lax.broadcasted_iota(jnp.int32, (8, n), 1)
    sub = lax.broadcasted_iota(jnp.int32, (8, n), 0)
    for p in range(n // w):
        lo = p * w
        rows = [[c[8 * g : 8 * g + 8] for g in groups] for c in cur]
        unit = [[(lane == sub + (lo + 8 * g)).astype(f32) for g in groups] for _ in mats]
        upper = [[] for _ in mats]
        inner = [[] for _ in mats]
        for k in range(0, w, part):
            col = [
                [
                    [jnp.broadcast_to(f[g][:, lo + t : lo + t + 1], (8, n)) for g in groups]
                    for t in range(k, k + part)
                ]
                for f in rows
            ]
            for t in range(k, k + part):
                tg, tr = t // 8, t % 8
                below = range((t + 1) // 8, w // 8)
                for q in many:
                    c = col[q][t - k]
                    r = lax.rsqrt(c[tg][tr : tr + 1])
                    rp = r * r
                    row = rows[q][tg][tr : tr + 1]
                    one = unit[q][tg][tr : tr + 1]
                    upper[q].append(row * r)
                    inner[q].append(one * r)
                    for v in range(t + 1, k + part):
                        e = c[v // 8][v % 8 : v % 8 + 1]
                        for g in below:
                            if 8 * g + 7 >= v:
                                col[q][v - k][g] = col[q][v - k][g] - (c[g] * e) * rp
                    row, one = row * rp, one * rp
                    for g in below:
                        rows[q][g] = rows[q][g] - c[g] * row
                        unit[q][g] = unit[q][g] - c[g] * one
        at = lane[:1]
        inside = (at >= lo) & (at < lo + w)
        for q in many:
            u = jnp.concatenate(upper[q], axis=0)
            y = jnp.where(inside, jnp.concatenate(inner[q], axis=0), u)
            out[q].append(jnp.where(at < lo + w, y, 0.0))
            if lo + w < n:
                uh, ul = split(u)
                yh, yl = split(y)
                term = lax.dot_general(
                    jnp.concatenate([uh, ul, uh], axis=0),
                    jnp.concatenate([yh, yh, yl], axis=0),
                    (((0,), (0,)), ((), ())),
                    preferred_element_type=f32,
                )
                cur[q] = jnp.where(inside, 0.0, cur[q][w:]) - term[lo + w :]
        for _ in range(steps):
            if beside:
                beside.pop(0)()
    return [jnp.concatenate(o, axis=0) for o in out]


class Boxes:
    def __init__(self, sides):
        self.sides = sides
        self.kept = {}

    def row(self, c, n):
        return self.sides[c[1]][c[0] + 1, BLK + n : BLK + n + 1, :]

    def once(self, key, make):
        if key not in self.kept:
            self.kept[key] = make()
        return self.kept[key]

    def interp(self, c):
        return self.once(("i", c), lambda: split(self.sides[c[1]][c[0] + 1, :BLK, :]))

    def interp_t(self, c):
        return self.once(("t", c), lambda: split(self.sides[c[1]][c[0] + 1, :BLK, :].T))

    def place(self, c, n):
        value = self.row(c, n) * scale
        if n < 2 and c != OWN:
            value = value + (1.0 - self.row(c, 6)) * (1e6 * (1 + idx(*c)))
        return value

    def col(self, c, n):
        return self.once(("c", c, n), lambda: column_of(self.place(c, n)))

    def kernel(self, c, part, m, part_m):
        value = kap(
            self.col(c, part), self.col(c, 2 + part), self.place(m, part_m), self.place(m, 2 + part_m)
        )
        if c == m and part == part_m:
            weight = self.row(c, 4 + part) + (1.0 - self.row(c, 6))
            value = value + jnp.where(eye(BLK), weight, 0.0)
        return value

    def rows_of(self, c, wanted):
        result = {}
        for work in self.rows_later(result, c, wanted):
            work()
        return result

    def rows_later(self, result, c, wanted):
        wanted = list(wanted)

        def work(pair):
            skel = jnp.concatenate([self.kernel(c, 0, m, p) for m, p in pair], axis=1)
            red = jnp.concatenate([self.kernel(c, 1, m, p) for m, p in pair], axis=1)
            value = red - dot_pair(self.interp_t(c), split(skel))
            for k, key in enumerate(pair):
                result[key] = value[:, k * BLK : (k + 1) * BLK]

        return [functools.partial(work, wanted[n : n + 2]) for n in range(0, len(wanted), 2)]


def reduced(pair, interp):
    return pair[1] - dot_pair(split(pair[0]), interp)


class Factor(dict):
    def __init__(self, *args):
        super().__init__(*args)
        self.kept = {}

    def halves(self, key):
        if key not in self.kept:
            self.kept[key] = split(self[key])
        return self.kept[key]


def subtract_fill(rows, factor_e, at, interp, keys):
    gain = factor_e[at, 1] - dot_pair(factor_e.halves((at, 0)), interp)
    gain = split(gain.T)
    keys = [k for k in keys if k in rows]
    for n in range(0, len(keys), 2):
        pair = keys[n : n + 2]
        parts = [factor_e.halves(k) for k in pair]
        both = [jnp.concatenate([p[i] for p in parts], axis=1) for i in range(2)]
        value = dot_pair(gain, both)
        for k, key in enumerate(pair):
            rows[key] = rows[key] - value[:, k * BLK : (k + 1) * BLK]


def solve(rows_list, centres, interps, beside=()):
    mats = [reduced((r[c, 0], r[c, 1]), i) for r, c, i in zip(rows_list, centres, interps)]
    inverses = [split(u) for u in factor(mats, list(beside))]
    results = []
    for rows, centre, inv in zip(rows_list, centres, inverses):
        keys = [k for k in rows if k != (centre, 1)]
        result = Factor()
        for n in range(0, len(keys), 2):
            pair = keys[n : n + 2]
            value = dot_pair(inv, split(jnp.concatenate([rows[k] for k in pair], axis=1)))
            for k, key in enumerate(pair):
                result[key] = value[:, k * BLK : (k + 1) * BLK]
        results.append(result)
    return results


OWN = (0, 0)
ALL_SKEL = [(m, 0) for m in OFFS]


def own_solution(boxes, rows):
    return solve([rows], [OWN], [boxes.interp(OWN)])[0]


def colour_0(boxes):
    return own_solution(boxes, boxes.rows_of(OWN, ALL_SKEL + [(OWN, 1)]))


def colour_1(boxes):
    sources = [(0, b) for b in (-1, 1)]
    wanted = [
        [(OWN, 0), (OWN, 1), ((-1, 0), 0), ((1, 0), 0)]
        + [((a, b), 0) for a in (-1, 0, 1)]
        + [((0, b), 1)]
        for _, b in sources
    ]
    first = first_factors(boxes, sources, wanted)
    own = boxes.rows_of(OWN, ALL_SKEL + [(OWN, 1)])
    for f in first.values():
        subtract_fill(own, f, OWN, boxes.interp(OWN), f.keys())
    return own_solution(boxes, own)


def colour_2(boxes):
    sources = [(a, 0) for a in (-1, 1)]
    wanted = [
        [((0, b), p) for b in (-1, 0, 1) for p in (0, 1)]
        + [((a, b), 0) for b in (-1, 0, 1)]
        + [((a, 0), 1)]
        for a, _ in sources
    ]
    first = first_factors(boxes, sources, wanted)
    own = boxes.rows_of(OWN, ALL_SKEL + [((0, b), 1) for b in (-1, 0, 1)])
    for f in first.values():
        subtract_fill(own, f, OWN, boxes.interp(OWN), f.keys())
    return own


def colour_3(boxes):
    sources = [(a, b) for a in (-1, 1) for b in (-1, 1)]
    wanted = [
        [(m, p) for m in (OWN, (a, 0), (0, b), (a, b)) for p in (0, 1)] for a, b in sources
    ]
    second_at = [(-1, 0), (1, 0)]
    rows = [{} for _ in second_at]
    beside = []
    for (a, _), part in zip(second_at, rows):
        keys = [((a, 0), 0), ((a, 0), 1), (OWN, 0), (OWN, 1)]
        keys += [((0, b), p) for b in (-1, 1) for p in (0, 1)]
        keys += [((a, b), 0) for b in (-1, 1)]
        beside += boxes.rows_later(part, (a, 0), keys)
    first = first_factors(boxes, sources, wanted, beside)
    for (a, _), part in zip(second_at, rows):
        for b in (-1, 1):
            f = first[a, b]
            subtract_fill(part, f, (a, 0), boxes.interp((a, 0)), f.keys())
    own = {}
    beside = boxes.rows_later(own, OWN, ALL_SKEL + [(OWN, 1)])
    for f in first.values():
        beside.append(
            functools.partial(subtract_fill, own, f, OWN, boxes.interp(OWN), f.keys())
        )
    second = solve(rows, second_at, [boxes.interp(c) for c in second_at], beside)
    for f in second:
        subtract_fill(own, f, OWN, boxes.interp(OWN), f.keys())
    return own, second


def first_factors(boxes, sources, wanted, beside=()):
    found = solve(
        [boxes.rows_of(c, k) for c, k in zip(sources, wanted)],
        sources,
        [boxes.interp(c) for c in sources],
        beside,
    )
    return dict(zip(sources, found))


def early_kernel(colour, mid, left, right, f_ref):
    boxes = Boxes({0: mid, -1: left, 1: right})
    for mine, work in ((0, colour_0), (1, colour_1)):

        @pl.when(colour[0] == mine)
        def _(work=work):
            result = work(boxes)
            for m in OFFS:
                f_ref[idx(*m)] = result[m, 0]

        boxes.kept.clear()


def rows_kernel_2(colour, mid, left, right, h_ref):
    @pl.when(colour[0] == 2)
    def _():
        own = colour_2(Boxes({0: mid, -1: left, 1: right}))
        for key, value in own.items():
            h_ref[slot(key)] = value


def rows_kernel_3(colour, mid, left, right, h_ref, to_left, to_right):
    @pl.when(colour[0] == 3)
    def _():
        boxes = Boxes({0: mid, -1: left, 1: right})
        own, second = colour_3(boxes)
        for b, ref in ((-1, to_left), (1, to_right)):
            total = {}
            at = (0, b)
            order = [((a, v), 0) for a in (-1, 0, 1) for v in (b, 0)] + [(at, 1), (OWN, 1)]
            for key in order:
                total[key] = jnp.zeros((BLK, BLK), f32)
            for f in second:
                subtract_fill(total, f, at, boxes.interp(at), f.keys())
            for n, key in enumerate(order):
                ref[n] = -total[key]
        for key, value in own.items():
            h_ref[slot(key)] = value


def slot(key):
    return idx(*key[0]) if key[1] == 0 else red_slot(key[0][1])


def red_slot(b):
    return {0: 9, -1: 10, 1: 11}[b]


def second_kernel(colour, *refs):
    @pl.when(colour[0] == 2)
    def _():
        second_work(*refs)


def second_work(h_ref, from_left, from_right, interp, f_ref, to_left, to_right):
    rows = {(m, 0): h_ref[idx(*m)] for m in OFFS}
    for b in (-1, 0, 1):
        rows[(0, b), 1] = h_ref[red_slot(b)]
    for b, ref in ((-1, from_left), (1, from_right)):
        order = [((a, v), 0) for a in (-1, 0, 1) for v in (0, b)] + [(OWN, 1), ((0, b), 1)]
        for n, key in enumerate(order):
            rows[key] = rows[key] - ref[n]
    result = solve([rows], [OWN], [split(interp[...])])[0]
    for m in OFFS:
        f_ref[idx(*m)] = result[m, 0]
    for b, ref in ((-1, to_left), (1, to_right)):
        for n, key in enumerate(
            [((a, v), 0) for a in (-1, 0, 1) for v in (0, b)] + [((0, b), 1)]
        ):
            ref[n] = result[key]


def side_blocks(values, to_left, to_right):
    for b, ref in ((-1, to_left), (1, to_right)):
        for n, m in enumerate([(a, v) for a in (-1, 0, 1) for v in (0, b)]):
            ref[n] = values[m]


def third_kernel(colour, early, second, *refs):
    for old, mine in ((early, colour[0] < 2), (second, colour[0] == 2)):

        @pl.when(mine)
        def _(old=old):
            values = {m: old[idx(*m)] for m in OFFS}
            for m in OFFS:
                refs[-3][idx(*m)] = values[m]
            side_blocks(values, *refs[-2:])

    @pl.when(colour[0] == 3)
    def _():
        third_work(*refs)


def third_work(h_ref, from_left, from_right, interp, f_ref, to_left, to_right):
    rows = {(m, 0): h_ref[idx(*m)] for m in OFFS}
    rows[OWN, 1] = h_ref[9]
    own_interp = split(interp[...])
    for b, ref in ((-1, from_left), (1, from_right)):
        f = Factor()
        for n, key in enumerate(
            [((a, v), 0) for a in (-1, 0, 1) for v in (b, 0)] + [(OWN, 1)]
        ):
            f[key] = ref[n]
        subtract_fill(rows, f, OWN, own_interp, f.keys())
    result = solve([rows], [OWN], [own_interp])[0]
    values = {m: result[m, 0] for m in OFFS}
    for m in OFFS:
        f_ref[idx(*m)] = values[m]
    side_blocks(values, to_left, to_right)


def sums_kernel(f_ref, from_left, from_right, t_ref, up_ref, down_ref):
    f = {OWN: {m: split(f_ref[idx(*m)]) for m in OFFS}}
    for b, ref in ((-1, from_left), (1, from_right)):
        f[0, b] = {
            m: split(ref[n]) for n, m in enumerate([(a, v) for a in (-1, 0, 1) for v in (b, 0)])
        }
    turned = {
        (e, a): tuple(x.T for x in split_f32(f_ref, from_left, from_right, e, a))
        for e in f
        for a in (-1, 0, 1)
    }
    for a, ref in ((-1, up_ref), (0, t_ref), (1, down_ref)):
        across = [m for m in OFFS if a == 0 or m[0] in (0, a)]
        for n, m in enumerate(across):
            total = None
            for e in f:
                if m in f[e]:
                    term = dot_pair(split(turned[e, a][0]), f[e][m])
                    total = term if total is None else total + term
            ref[n] = total


def split_f32(f_ref, from_left, from_right, e, a):
    if e == OWN:
        return (f_ref[idx(a, 0)],)
    ref = from_left if e[1] < 0 else from_right
    return (ref[2 * (a + 1) + 1],)


def turned_pieces(total, below, above, details, wanted):
    mine = {}
    for n in wanted:
        value = total[n]
        if n >= 3:
            value = value + below[n - 3]
        if n < 6:
            value = value + above[n]
        value = -value
        if n == 4:
            value = value + jnp.where(eye(BLK), details[4:5, :], 0.0)
        mine[n] = value.T
    return mine


def gather(piece, start, tiles, per, at, width):
    return [
        piece[start + t * per : start + (t + 1) * per, at : at + width] for t in range(tiles)
    ]


def pack_lead(lead_per, per, total, below, above, details, lead_ref):
    mine = turned_pieces(total, below, above, details, HALF)
    for s, n in enumerate(HALF):
        piece = gather(mine[n], 0, lead_per // per, per, 0, lead_per)
        piece = jnp.concatenate(piece, axis=1) * (0.5 if n == 4 else 1.0)
        for d in range(lead_ref.shape[0]):
            lead_ref[d, s * per : (s + 1) * per, :] = piece


def pack_rest(lead_per, row_per, col_per, per, place, total, below, above, details, x_ref, yo_ref):
    mine = turned_pieces(total, below, above, details, ALL)
    tiles = lead_per // per
    grid_rows, grid_cols = yo_ref.shape[:2]
    for n in range(9):
        at = slice(n * per, (n + 1) * per)
        for_col = [gather(mine[n], 0, tiles, per, q * col_per, col_per) for q in range(grid_cols)]
        for r in range(grid_rows):
            d = lax.rem(r - place[2] + grid_rows, grid_rows)
            for_row = gather(mine[n], 0, tiles, per, r * row_per, row_per)
            x_ref[d, at, :] = jnp.concatenate(for_row, axis=1)
            for q in range(grid_cols):
                for_tile = gather(
                    mine[n], q * col_per, col_per // per, per, r * row_per, row_per
                )
                yo_ref[r, q, at, :] = jnp.concatenate(for_col[q] + for_tile, axis=1)


HALF = (4, 5, 6, 7, 8)
ALL = tuple(range(9))


def assemble(source, offsets, boxes, per, height, tiles, out_ref, base, grid_cols, near):
    depth = len(offsets) * per
    r = lax.broadcasted_iota(jnp.int32, (depth, TILE), 0)
    c = lax.broadcasted_iota(jnp.int32, (depth, TILE), 1)
    n, inner = r // per + offsets[0], r % per
    box = c % boxes
    same = inner == c // boxes
    box_row, box_col = box // grid_cols - (n // 3 - 1), box % grid_cols - (n % 3 - 1)

    def group(g, carry):
        values = []
        for s in range(8):
            b = g * 8 + s
            hot = same & (box_row == b // grid_cols) & (box_col == b % grid_cols)
            hot = hot.astype(f32).astype(bf16)
            hi, lo = split(source(b))
            values.append(dot(hi, hot) + dot(lo, hot))
        for t in range(tiles):
            part = jnp.stack([v[t * height : (t + 1) * height] for v in values], axis=0)
            part = jnp.swapaxes(part, 0, 1)
            across = slice(t * TILE, (t + 1) * TILE)
            for k in range(height):
                at = pl.ds(pl.multiple_of(base + k * boxes + g * 8, 8), 8)
                out_ref[at, across] = part[k] if near is None else part[k] + near[at, across]
        return carry

    lax.fori_loop(0, boxes // 8, group, 0)


def near_kernel(lead_pts, xy_pts, row_pts, col_pts, lead_ref, xy_ref, own_ref):
    def fill(row_ref, col_ref, out_ref, upper):
        def body(i, carry):
            at = pl.ds(pl.multiple_of(i * BLK, BLK), BLK)
            cx = column_of(row_ref[0:1, at] * scale)
            cy = column_of(row_ref[1:2, at] * scale)
            for j in range(out_ref.shape[1] // BLK):
                there = slice(j * BLK, (j + 1) * BLK)

                def work(there=there):
                    out_ref[at, there] = kap(
                        cx, cy, col_ref[0:1, there] * scale, col_ref[1:2, there] * scale
                    )

                if upper:
                    pl.when(j >= i)(work)
                else:
                    work()
            return carry

        lax.fori_loop(0, out_ref.shape[0] // BLK, body, 0)

    fill(lead_pts, lead_pts, lead_ref, True)
    fill(xy_pts, lead_pts, xy_ref, False)
    fill(row_pts, col_pts, own_ref, False)


def lead_first(grid_cols, pack_ref, near, uh_ref, ul_ref, ih_ref, il_ref, rest_ref, mat, half):
    size = mat.shape[0]
    boxes = pack_ref.shape[0]
    per = TILE // boxes
    assemble(
        lambda b: pack_ref[b].T,
        HALF,
        boxes,
        per,
        size // boxes,
        size // TILE,
        half,
        0,
        grid_cols,
        None,
    )
    for i in range(size // BLK):
        here = slice(i * BLK, (i + 1) * BLK)
        for j in range(i, size // BLK):
            there = slice(j * BLK, (j + 1) * BLK)
            mat[here, there] = half[here, there] + half[there, here].T + near[here, there]
    lead_steps(mat, uh_ref, ul_ref, ih_ref, il_ref)
    done = uh_ref.shape[0]
    rest_ref[...] = mat[done:, done:]


def lead_second(rest_ref, uh_ref, ul_ref, ih_ref, il_ref, mat):
    mat[...] = rest_ref[...]
    lead_steps(mat, uh_ref, ul_ref, ih_ref, il_ref)


def lead_steps(mat, uh_ref, ul_ref, ih_ref, il_ref):
    pair = 2 * BLK
    count = mat.shape[0] // pair

    def step(p, carry):
        both = pl.ds(pl.multiple_of(p * pair, pair), pair)
        a = pl.ds(pl.multiple_of(p * pair, BLK), BLK)
        b = pl.ds(pl.multiple_of(p * pair + BLK, BLK), BLK)
        inv_a = factor([mat[a, a]])[0]
        split_a = split(inv_a)
        between = dot_pair(split_a, split(mat[a, b]))
        turned = split(between.T)
        inv_b = factor([mat[b, b] - dot_pair(turned, split(between))])[0]
        corner = -dot_pair(split(inv_b), split(dot_pair(turned, split_a)))
        inv = jnp.concatenate(
            [
                jnp.concatenate([inv_a, jnp.zeros((BLK, BLK), f32)], axis=1),
                jnp.concatenate([corner, inv_b], axis=1),
            ],
            axis=0,
        )
        ih_ref[both, :], il_ref[both, :] = split(inv.T)
        for i in range(min(uh_ref.shape[0] // pair, count - 1)):

            @pl.when(p == i)
            def _(i=i):
                here = slice(i * pair, (i + 1) * pair)
                row = dot_pair(split(inv), split(mat[here, (i + 1) * pair :]))
                hi, lo = split(row)
                uh_ref[here, (i + 1) * pair :] = hi
                ul_ref[here, (i + 1) * pair :] = lo
                for j in range(i + 1, count):
                    at = (j - i - 1) * pair
                    left = split(row[:, at : at + pair].T)
                    rows = slice(j * pair, (j + 1) * pair)
                    mat[rows, j * pair :] = mat[rows, j * pair :] - dot_pair(
                        left, (hi[:, at:], lo[:, at:])
                    )

        return carry

    lax.fori_loop(0, uh_ref.shape[0] // pair, step, 0)


def tile_kernel(
    grid_cols,
    place,
    x_half,
    x_other,
    rest,
    near_xy,
    near_own,
    uh_first,
    ul_first,
    uh_second,
    ul_second,
    ih_first,
    il_first,
    ih_second,
    il_second,
    out_ref,
    mat,
    ph,
    plo,
    sems,
):
    total, size = mat.shape
    rows, cols = out_ref.shape
    boxes = rest.shape[0]
    per = TILE // boxes
    tiles = size // TILE
    row_per, col_per = rows // boxes, cols // boxes
    ends = [0, tiles * col_per]
    ends.append(ends[1] + cols // TILE * row_per)

    def part(n):
        return lambda b: rest[b].T[ends[n] : ends[n + 1]]

    def from_row(b):
        grid_rows = x_half.shape[1]
        d = lax.rem(place[2] - b // grid_cols + grid_rows, grid_rows)
        side = lax.bitwise_xor(place[3], b % grid_cols)
        k = side // 2
        odd = jnp.full((1, 1), side % 2, jnp.int32) == 1
        return jnp.where(odd, x_other[k, d], x_half[k, d]).T

    copies = [
        pltpu.make_async_copy(near_xy.at[:rows], mat.at[:rows], sems.at[0]),
        pltpu.make_async_copy(near_xy.at[rows:], mat.at[rows:], sems.at[1]),
        pltpu.make_async_copy(near_own, out_ref, sems.at[2]),
    ]
    for copy in copies:
        copy.start()
    copies[0].wait()
    assemble(from_row, ALL, boxes, per, row_per, tiles, mat, 0, grid_cols, mat)
    copies[1].wait()
    assemble(part(0), ALL, boxes, per, col_per, tiles, mat, rows, grid_cols, mat)
    pair = 2 * BLK
    chunk = 4 * BLK
    middle = uh_first.shape[0]

    def solve_rows(c, carry):
        at = pl.ds(pl.multiple_of(c * chunk, chunk), chunk)
        for p in range(size // pair):
            here = slice(p * pair, (p + 1) * pair)
            acc = mat[at, here]
            edge = min(p * pair, middle)
            if p > 0:
                acc = acc - dot_pair(
                    (ph[at, :edge], plo[at, :edge]), (uh_first[:edge, here], ul_first[:edge, here])
                )
            if p * pair > middle:
                before, above = slice(middle, p * pair), slice(0, p * pair - middle)
                across = slice(p * pair - middle, (p + 1) * pair - middle)
                acc = acc - dot_pair(
                    (ph[at, before], plo[at, before]),
                    (uh_second[above, across], ul_second[above, across]),
                )
            if p * pair < middle:
                inv = ih_first[here, :], il_first[here, :]
            else:
                across = slice(p * pair - middle, (p + 1) * pair - middle)
                inv = ih_second[across, :], il_second[across, :]
            value = dot_pair(split(acc), inv)
            mat[at, here] = value
            hi, lo = split(value)
            ph[at, here] = hi
            plo[at, here] = lo
        return carry

    lax.fori_loop(0, total // chunk, solve_rows, 0)
    copies[2].wait()
    first_row, first_col = place[0], place[1]

    @pl.when(first_col < size)
    def _():
        r = first_row + lax.broadcasted_iota(jnp.int32, (rows, cols), 0)
        c = first_col + lax.broadcasted_iota(jnp.int32, (rows, cols), 1)
        start = pl.multiple_of(first_col, BLK)
        out_ref[...] = jnp.where(r >= c, mat[:rows, pl.ds(start, cols)], 0.0)

    @pl.when(first_col >= size)
    def _():
        assemble(
            part(1), ALL, boxes, per, row_per, cols // TILE, out_ref, 0, grid_cols, out_ref
        )

        def update(c, carry):
            at = pl.ds(pl.multiple_of(c * chunk, chunk), chunk)
            value = out_ref[at, :] - dot_pair(
                (ph[at, :], plo[at, :]), (ph[rows:, :], plo[rows:, :]), nt=True
            )
            r = first_row + c * chunk + lax.broadcasted_iota(jnp.int32, (chunk, cols), 0)
            out_ref[at, :] = jnp.where(r >= size, value, 0.0)
            return carry

        lax.fori_loop(0, rows // chunk, update, 0)


def blocks(*counts):
    return [jax.ShapeDtypeStruct((n, BLK, BLK), f32) for n in counts]


def on_device(offsets, point_order, nugget, interp):
    row_at = lax.axis_index("row")
    col_at = lax.axis_index("col")
    row_count = lax.axis_size("row")
    col_count = lax.axis_size("col")
    box_total = row_count * col_count
    skel = interp.shape[2]
    box_id = row_at * col_count + col_at
    both = ("row", "col")

    corner = jnp.stack([row_at, col_at]).astype(f32)[:, None]
    table = jnp.concatenate([offsets[0, 0] + corner, nugget[0, 0][None]], axis=0)
    table = jnp.take(table, point_order[0, 0], axis=1)
    details = jnp.concatenate(
        [table.reshape(6, BLK), jnp.ones((1, BLK), f32), jnp.zeros((1, BLK), f32)], axis=0
    )
    packed = jnp.concatenate([interp[0, 0], details], axis=0)
    skeleton = jnp.concatenate([table[:2, :skel], jnp.zeros((6, skel), f32)], axis=0)
    def exchange(x):
        return lax.all_to_all(x, both, split_axis=0, concat_axis=0, tiled=True)

    def hop(x, axis, distance):
        count = lax.axis_size(axis)
        return lax.ppermute(
            x, axis, [(i, i + distance) for i in range(count) if 0 <= i + distance < count]
        )

    def side_hop(x, distance, row_odd, col_odd):
        pairs = [
            (i * col_count + j, i * col_count + j + distance)
            for i in range(row_count)
            for j in range(col_count)
            if i % 2 == row_odd and j % 2 == col_odd and 0 <= j + distance < col_count
        ]
        return lax.ppermute(x, both, pairs)

    mid = jnp.stack([hop(packed, "row", 1), packed, hop(packed, "row", -1)])
    left = hop(mid, "col", 1)
    right = hop(mid, "col", -1)
    colour = 2 * (row_at % 2) + col_at % 2

    flag = colour[None].astype(jnp.int32)
    own_interp = interp[0, 0]

    def local(kernel, counts, name, *args):
        vmem = pl.BlockSpec(memory_space=pltpu.VMEM)
        return pl.pallas_call(
            kernel,
            in_specs=[pl.BlockSpec(memory_space=pltpu.SMEM)] + [vmem] * len(args),
            out_shape=blocks(*counts),
            compiler_params=VMEM,
            name=name,
        )(flag, *args)

    rows_3, pay_left, pay_right = local(rows_kernel_3, (10, 8, 8), "rows_3", mid, left, right)
    from_right = side_hop(pay_left, -1, 1, 1)
    from_left = side_hop(pay_right, 1, 1, 1)
    mid, left, right, rows_3 = lax.optimization_barrier((mid, left, right, rows_3))
    (rows_2,) = local(rows_kernel_2, (12,), "rows_2", mid, left, right)
    mid, left, right, rows_2, skeleton = lax.optimization_barrier(
        (mid, left, right, rows_2, skeleton)
    )
    everyone = exchange(jnp.broadcast_to(skeleton[None], (box_total,) + skeleton.shape))
    (early,) = local(early_kernel, (9,), "early", mid, left, right)
    second, pay_left, pay_right = local(
        second_kernel, (9, 7, 7), "second", rows_2, from_left, from_right, own_interp
    )
    from_right = side_hop(pay_left, -1, 1, 0)
    from_left = side_hop(pay_right, 1, 1, 0)
    f_own, pay_left, pay_right = local(
        third_kernel,
        (9, 6, 6),
        "third",
        early,
        second,
        rows_3,
        from_left,
        from_right,
        own_interp,
    )
    from_right = hop(pay_left, "col", -1)
    from_left = hop(pay_right, "col", 1)
    total, up, down = pl.pallas_call(
        sums_kernel, out_shape=blocks(9, 6, 6), compiler_params=VMEM, name="sums"
    )(f_own, from_left, from_right)
    from_below = hop(up, "row", -1)
    from_above = hop(down, "row", 1)
    lead = PANELS * PW
    lead_per = lead // box_total
    row_per = skel // row_count
    col_per = skel // col_count
    per = TILE // box_total
    lead_tiles = lead_per // per
    lanes = lead_tiles * col_per + col_per // per * row_per
    points = jnp.transpose(everyone[:, :2], (1, 2, 0))

    def flat(x):
        return jnp.pad(x.reshape(2, -1), ((0, 6), (0, 0)))

    lead_pts = flat(points[:, :lead_per])
    row_pts = lax.dynamic_slice_in_dim(points, row_at * row_per, row_per, 1)
    col_pts = lax.dynamic_slice_in_dim(points, col_at * col_per, col_per, 1)
    xy_pts = flat(jnp.concatenate([row_pts, col_pts], axis=1))
    row_pts, col_pts = flat(row_pts), flat(col_pts)
    rows_here = row_per * box_total
    cols_here = col_per * box_total
    both_rows = rows_here + cols_here
    total, lead_pts, xy_pts, row_pts, col_pts = lax.optimization_barrier(
        (total, lead_pts, xy_pts, row_pts, col_pts)
    )
    sums = total, from_below, from_above, details
    lead_piece = pl.pallas_call(
        functools.partial(pack_lead, lead_per, per),
        out_shape=jax.ShapeDtypeStruct(
            (box_total, len(HALF) * per, lead_tiles * lead_per), f32
        ),
        compiler_params=VMEM,
        name="pack_lead",
    )(*sums)
    lead_pack = exchange(lead_piece)
    lead_piece, sums, *pts = lax.optimization_barrier(
        (lead_piece, sums, lead_pts, xy_pts, row_pts, col_pts)
    )
    place = jnp.stack([row_at * rows_here, col_at * cols_here, row_at, col_at]).astype(jnp.int32)
    vmem = pl.BlockSpec(memory_space=pltpu.VMEM)
    smem = pl.BlockSpec(memory_space=pltpu.SMEM)
    for_rows, rest = pl.pallas_call(
        functools.partial(pack_rest, lead_per, row_per, col_per, per),
        in_specs=[smem] + [vmem] * 4,
        out_shape=[
            jax.ShapeDtypeStruct((row_count, 9 * per, lead_tiles * row_per), f32),
            jax.ShapeDtypeStruct((row_count, col_count, 9 * per, lanes), f32),
        ],
        compiler_params=VMEM,
        name="pack_rest",
    )(place, *sums)
    x_rows = jnp.stack(
        [for_rows[0]]
        + [
            lax.ppermute(for_rows[d], "row", [(i, (i + d) % row_count) for i in range(row_count)])
            for d in range(1, row_count)
        ]
    )
    near_lead, near_xy, near_own = pl.pallas_call(
        near_kernel,
        out_shape=[
            jax.ShapeDtypeStruct((lead, lead), f32),
            jax.ShapeDtypeStruct((both_rows, lead), f32),
            jax.ShapeDtypeStruct((rows_here, cols_here), f32),
        ],
        compiler_params=VMEM,
        cost_estimate=pl.CostEstimate(
            flops=20 * lead * both_rows, bytes_accessed=12 * lead * both_rows, transcendentals=0
        ),
        name="near",
    )(*pts)
    rest, lead_pack, near_lead, x_rows = lax.optimization_barrier(
        (rest, lead_pack, near_lead, x_rows)
    )
    rest = exchange(rest.reshape(box_total, 9 * per, lanes))

    def swap(x, d):
        return lax.ppermute(x, "col", [(j, j ^ d) for j in range(col_count)])

    x_sides = [swap(x_rows, d) for d in range(2, col_count, 2)]
    middle = lead // 2

    def halves(rows, cols):
        return [jax.ShapeDtypeStruct((rows, cols), bf16)] * 2

    *first, remaining = pl.pallas_call(
        functools.partial(lead_first, col_count),
        out_shape=halves(middle, lead)
        + halves(middle, 2 * BLK)
        + [jax.ShapeDtypeStruct((lead - middle, lead - middle), f32)],
        scratch_shapes=[pltpu.VMEM((lead, lead), f32)] * 2,
        compiler_params=VMEM,
        name="lead_first",
    )(lead_pack, near_lead)
    remaining, x_sides, x_rows = lax.optimization_barrier((remaining, x_sides, x_rows))
    x_half = jnp.stack([x_rows] + x_sides)
    x_other = swap(x_half, 1)
    second = pl.pallas_call(
        lead_second,
        out_shape=halves(lead - middle, lead - middle) + halves(lead - middle, 2 * BLK),
        scratch_shapes=[pltpu.VMEM((lead - middle, lead - middle), f32)],
        compiler_params=VMEM,
        name="lead_second",
    )(remaining)
    return pl.pallas_call(
        functools.partial(tile_kernel, col_count),
        in_specs=[smem] + [vmem] * 3 + [pl.BlockSpec(memory_space=pl.ANY)] * 2 + [vmem] * 8,
        out_specs=vmem,
        out_shape=jax.ShapeDtypeStruct((rows_here, cols_here), f32),
        scratch_shapes=[
            pltpu.VMEM((both_rows, lead), f32),
            pltpu.VMEM((both_rows, lead), bf16),
            pltpu.VMEM((both_rows, lead), bf16),
            pltpu.SemaphoreType.DMA((3,)),
        ],
        compiler_params=VMEM,
        name="tile",
    )(
        place,
        x_half,
        x_other,
        rest,
        near_xy,
        near_own,
        *first[:2],
        *second[:2],
        *first[2:],
        *second[2:],
    )


def solution(mesh):
    in_specs = (
        P("row", "col", None, None),
        P("row", "col", None),
        P("row", "col", None),
        P("row", "col", None, None),
    )
    return jax.shard_map(
        on_device, mesh=mesh, in_specs=in_specs, out_specs=P("row", "col"), check_vma=False
    )
```

```python
import functools
import math

import jax
import jax.numpy as jnp
from jax import lax
from jax.experimental import pallas as pl
from jax.experimental.pallas import tpu as pltpu
from jax.sharding import PartitionSpec as P

PW = 512
PANELS = 2
kernel_amp = 0.015625
kernel_len = 0.5
scale = math.log2(math.e) / kernel_len
log_amp = math.log2(kernel_amp)
f32 = jnp.float32
bf16 = jnp.bfloat16
BLK = 128
TILE = 256
VMEM = pltpu.CompilerParams(vmem_limit_bytes=56 * 1024 * 1024)
OFFS = [(a, b) for a in (-1, 0, 1) for b in (-1, 0, 1)]


def idx(a, b):
    return (a + 1) * 3 + (b + 1)


def split(x):
    hi = x.astype(bf16)
    return hi, (x - hi.astype(f32)).astype(bf16)


def dot(a, b, nt=False):
    dims = ((1,), (1,)) if nt else ((1,), (0,))
    return lax.dot_general(a, b, (dims, ((), ())), preferred_element_type=f32)


def dot_pair(a, b, nt=False):
    left = jnp.concatenate([a[0], a[1], a[0]], axis=1)
    return dot(left, jnp.concatenate([b[0], b[0], b[1]], axis=1 if nt else 0), nt)


def dot3(a, b):
    return dot_pair(split(a), split(b))


def kap(cx, cy, rx, ry):
    dx = cx - rx
    dy = cy - ry
    d2 = dx * dx + dy * dy
    dist = d2 * lax.rsqrt(jnp.maximum(d2, 1e-30))
    return jnp.exp2(log_amp - dist)


def column_of(row):
    return jnp.broadcast_to(row, (BLK, BLK)).T


def eye(n):
    return lax.broadcasted_iota(jnp.int32, (n, n), 0) == lax.broadcasted_iota(
        jnp.int32, (n, n), 1
    )


def factor(mats, beside=()):
    n = mats[0].shape[0]
    w, part = (32, 16) if len(mats) == 1 else (16, 8)
    steps = -(-len(beside) * w // n)
    groups = range(w // 8)
    many = range(len(mats))
    cur = list(mats)
    out = [[] for _ in mats]
    lane = lax.broadcasted_iota(jnp.int32, (8, n), 1)
    sub = lax.broadcasted_iota(jnp.int32, (8, n), 0)
    for p in range(n // w):
        lo = p * w
        rows = [[c[8 * g : 8 * g + 8] for g in groups] for c in cur]
        unit = [[(lane == sub + (lo + 8 * g)).astype(f32) for g in groups] for _ in mats]
        upper = [[] for _ in mats]
        inner = [[] for _ in mats]
        for k in range(0, w, part):
            col = [
                [
                    [jnp.broadcast_to(f[g][:, lo + t : lo + t + 1], (8, n)) for g in groups]
                    for t in range(k, k + part)
                ]
                for f in rows
            ]
            for t in range(k, k + part):
                tg, tr = t // 8, t % 8
                below = range((t + 1) // 8, w // 8)
                for q in many:
                    c = col[q][t - k]
                    r = lax.rsqrt(c[tg][tr : tr + 1])
                    rp = r * r
                    row = rows[q][tg][tr : tr + 1]
                    one = unit[q][tg][tr : tr + 1]
                    upper[q].append(row * r)
                    inner[q].append(one * r)
                    for v in range(t + 1, k + part):
                        e = c[v // 8][v % 8 : v % 8 + 1]
                        for g in below:
                            if 8 * g + 7 >= v:
                                col[q][v - k][g] = col[q][v - k][g] - (c[g] * e) * rp
                    row, one = row * rp, one * rp
                    for g in below:
                        rows[q][g] = rows[q][g] - c[g] * row
                        unit[q][g] = unit[q][g] - c[g] * one
        at = lane[:1]
        inside = (at >= lo) & (at < lo + w)
        for q in many:
            u = jnp.concatenate(upper[q], axis=0)
            y = jnp.where(inside, jnp.concatenate(inner[q], axis=0), u)
            out[q].append(jnp.where(at < lo + w, y, 0.0))
            if lo + w < n:
                uh, ul = split(u)
                yh, yl = split(y)
                term = lax.dot_general(
                    jnp.concatenate([uh, ul, uh], axis=0),
                    jnp.concatenate([yh, yh, yl], axis=0),
                    (((0,), (0,)), ((), ())),
                    preferred_element_type=f32,
                )
                cur[q] = jnp.where(inside, 0.0, cur[q][w:]) - term[lo + w :]
        for _ in range(steps):
            if beside:
                beside.pop(0)()
    return [jnp.concatenate(o, axis=0) for o in out]


def order_kernel(corner, offsets, order, nugget, interp, out_ref):
    points = order.shape[1]
    table = jnp.concatenate(
        [
            offsets[0:1, :] + corner[0],
            offsets[1:2, :] + corner[1],
            nugget[...],
            jnp.zeros((13, points), f32),
        ],
        axis=0,
    )
    hot = lax.broadcasted_iota(jnp.int32, (points, points), 0) == order[...]
    hot = hot.astype(f32).astype(bf16)
    high, rest = table.astype(bf16), table
    rest = table - high.astype(f32)
    mid, low = split(rest)
    found = (dot(high, hot) + dot(mid, hot)) + dot(low, hot)
    skel = interp.shape[0]
    out_ref[:skel, :] = interp[...]
    parts = [found[i : i + 1, k : k + skel] for i in range(3) for k in (0, skel)]
    parts += [jnp.ones((1, skel), f32), jnp.zeros((1, skel), f32)]
    out_ref[skel:, :] = jnp.concatenate(parts, axis=0)


class Boxes:
    def __init__(self, sides):
        self.sides = sides
        self.kept = {}

    def row(self, c, n):
        return self.sides[c[1]][c[0] + 1, BLK + n : BLK + n + 1, :]

    def once(self, key, make):
        if key not in self.kept:
            self.kept[key] = make()
        return self.kept[key]

    def interp(self, c):
        return self.once(("i", c), lambda: split(self.sides[c[1]][c[0] + 1, :BLK, :]))

    def interp_t(self, c):
        return self.once(("t", c), lambda: split(self.sides[c[1]][c[0] + 1, :BLK, :].T))

    def place(self, c, n):
        value = self.row(c, n) * scale
        if n < 2 and c != OWN:
            value = value + (1.0 - self.row(c, 6)) * (1e6 * (1 + idx(*c)))
        return value

    def col(self, c, n):
        return self.once(("c", c, n), lambda: column_of(self.place(c, n)))

    def kernel(self, c, part, m, part_m):
        value = kap(
            self.col(c, part), self.col(c, 2 + part), self.place(m, part_m), self.place(m, 2 + part_m)
        )
        if c == m and part == part_m:
            weight = self.row(c, 4 + part) + (1.0 - self.row(c, 6))
            value = value + jnp.where(eye(BLK), weight, 0.0)
        return value

    def rows_of(self, c, wanted):
        result = {}
        for work in self.rows_later(result, c, wanted):
            work()
        return result

    def rows_later(self, result, c, wanted):
        wanted = list(wanted)

        def work(pair):
            skel = jnp.concatenate([self.kernel(c, 0, m, p) for m, p in pair], axis=1)
            red = jnp.concatenate([self.kernel(c, 1, m, p) for m, p in pair], axis=1)
            value = red - dot_pair(self.interp_t(c), split(skel))
            for k, key in enumerate(pair):
                result[key] = value[:, k * BLK : (k + 1) * BLK]

        return [functools.partial(work, wanted[n : n + 2]) for n in range(0, len(wanted), 2)]


def reduced(pair, interp):
    return pair[1] - dot_pair(split(pair[0]), interp)


class Factor(dict):
    def __init__(self, *args):
        super().__init__(*args)
        self.kept = {}

    def halves(self, key):
        if key not in self.kept:
            self.kept[key] = split(self[key])
        return self.kept[key]


def subtract_fill(rows, factor_e, at, interp, keys):
    gain = factor_e[at, 1] - dot_pair(factor_e.halves((at, 0)), interp)
    gain = split(gain.T)
    keys = [k for k in keys if k in rows]
    for n in range(0, len(keys), 2):
        pair = keys[n : n + 2]
        parts = [factor_e.halves(k) for k in pair]
        both = [jnp.concatenate([p[i] for p in parts], axis=1) for i in range(2)]
        value = dot_pair(gain, both)
        for k, key in enumerate(pair):
            rows[key] = rows[key] - value[:, k * BLK : (k + 1) * BLK]


def solve(rows_list, centres, interps, beside=()):
    mats = [reduced((r[c, 0], r[c, 1]), i) for r, c, i in zip(rows_list, centres, interps)]
    inverses = [split(u) for u in factor(mats, list(beside))]
    results = []
    for rows, centre, inv in zip(rows_list, centres, inverses):
        keys = [k for k in rows if k != (centre, 1)]
        result = Factor()
        for n in range(0, len(keys), 2):
            pair = keys[n : n + 2]
            value = dot_pair(inv, split(jnp.concatenate([rows[k] for k in pair], axis=1)))
            for k, key in enumerate(pair):
                result[key] = value[:, k * BLK : (k + 1) * BLK]
        results.append(result)
    return results


OWN = (0, 0)
ALL_SKEL = [(m, 0) for m in OFFS]


def own_solution(boxes, rows):
    return solve([rows], [OWN], [boxes.interp(OWN)])[0]


def colour_0(boxes):
    return own_solution(boxes, boxes.rows_of(OWN, ALL_SKEL + [(OWN, 1)]))


def colour_1(boxes):
    sources = [(0, b) for b in (-1, 1)]
    wanted = [
        [(OWN, 0), (OWN, 1), ((-1, 0), 0), ((1, 0), 0)]
        + [((a, b), 0) for a in (-1, 0, 1)]
        + [((0, b), 1)]
        for _, b in sources
    ]
    first = first_factors(boxes, sources, wanted)
    own = boxes.rows_of(OWN, ALL_SKEL + [(OWN, 1)])
    for f in first.values():
        subtract_fill(own, f, OWN, boxes.interp(OWN), f.keys())
    return own_solution(boxes, own)


def colour_2(boxes):
    sources = [(a, 0) for a in (-1, 1)]
    wanted = [
        [((0, b), p) for b in (-1, 0, 1) for p in (0, 1)]
        + [((a, b), 0) for b in (-1, 0, 1)]
        + [((a, 0), 1)]
        for a, _ in sources
    ]
    first = first_factors(boxes, sources, wanted)
    own = boxes.rows_of(OWN, ALL_SKEL + [((0, b), 1) for b in (-1, 0, 1)])
    for f in first.values():
        subtract_fill(own, f, OWN, boxes.interp(OWN), f.keys())
    return own


def colour_3(boxes):
    sources = [(a, b) for a in (-1, 1) for b in (-1, 1)]
    wanted = [
        [(m, p) for m in (OWN, (a, 0), (0, b), (a, b)) for p in (0, 1)] for a, b in sources
    ]
    second_at = [(-1, 0), (1, 0)]
    rows = [{} for _ in second_at]
    beside = []
    for (a, _), part in zip(second_at, rows):
        keys = [((a, 0), 0), ((a, 0), 1), (OWN, 0), (OWN, 1)]
        keys += [((0, b), p) for b in (-1, 1) for p in (0, 1)]
        keys += [((a, b), 0) for b in (-1, 1)]
        beside += boxes.rows_later(part, (a, 0), keys)
    first = first_factors(boxes, sources, wanted, beside)
    for (a, _), part in zip(second_at, rows):
        for b in (-1, 1):
            f = first[a, b]
            subtract_fill(part, f, (a, 0), boxes.interp((a, 0)), f.keys())
    own = {}
    beside = boxes.rows_later(own, OWN, ALL_SKEL + [(OWN, 1)])
    for f in first.values():
        beside.append(
            functools.partial(subtract_fill, own, f, OWN, boxes.interp(OWN), f.keys())
        )
    second = solve(rows, second_at, [boxes.interp(c) for c in second_at], beside)
    for f in second:
        subtract_fill(own, f, OWN, boxes.interp(OWN), f.keys())
    return own, second


def first_factors(boxes, sources, wanted, beside=()):
    found = solve(
        [boxes.rows_of(c, k) for c, k in zip(sources, wanted)],
        sources,
        [boxes.interp(c) for c in sources],
        beside,
    )
    return dict(zip(sources, found))


def early_kernel(colour, mid, left, right, f_ref):
    boxes = Boxes({0: mid, -1: left, 1: right})
    for mine, work in ((0, colour_0), (1, colour_1)):

        @pl.when(colour[0] == mine)
        def _(work=work):
            result = work(boxes)
            for m in OFFS:
                f_ref[idx(*m)] = result[m, 0]

        boxes.kept.clear()


def rows_kernel_2(colour, mid, left, right, h_ref):
    @pl.when(colour[0] == 2)
    def _():
        own = colour_2(Boxes({0: mid, -1: left, 1: right}))
        for key, value in own.items():
            h_ref[slot(key)] = value


def rows_kernel_3(colour, mid, left, right, h_ref, to_left, to_right):
    @pl.when(colour[0] == 3)
    def _():
        boxes = Boxes({0: mid, -1: left, 1: right})
        own, second = colour_3(boxes)
        for b, ref in ((-1, to_left), (1, to_right)):
            total = {}
            at = (0, b)
            order = [((a, v), 0) for a in (-1, 0, 1) for v in (b, 0)] + [(at, 1), (OWN, 1)]
            for key in order:
                total[key] = jnp.zeros((BLK, BLK), f32)
            for f in second:
                subtract_fill(total, f, at, boxes.interp(at), f.keys())
            for n, key in enumerate(order):
                ref[n] = -total[key]
        for key, value in own.items():
            h_ref[slot(key)] = value


def slot(key):
    return idx(*key[0]) if key[1] == 0 else red_slot(key[0][1])


def red_slot(b):
    return {0: 9, -1: 10, 1: 11}[b]


def second_kernel(colour, *refs):
    @pl.when(colour[0] == 2)
    def _():
        second_work(*refs)


def second_work(h_ref, from_left, from_right, interp, f_ref, to_left, to_right):
    rows = {(m, 0): h_ref[idx(*m)] for m in OFFS}
    for b in (-1, 0, 1):
        rows[(0, b), 1] = h_ref[red_slot(b)]
    for b, ref in ((-1, from_left), (1, from_right)):
        order = [((a, v), 0) for a in (-1, 0, 1) for v in (0, b)] + [(OWN, 1), ((0, b), 1)]
        for n, key in enumerate(order):
            rows[key] = rows[key] - ref[n]
    result = solve([rows], [OWN], [split(interp[...])])[0]
    for m in OFFS:
        f_ref[idx(*m)] = result[m, 0]
    for b, ref in ((-1, to_left), (1, to_right)):
        for n, key in enumerate(
            [((a, v), 0) for a in (-1, 0, 1) for v in (0, b)] + [((0, b), 1)]
        ):
            ref[n] = result[key]


def side_blocks(values, to_left, to_right):
    for b, ref in ((-1, to_left), (1, to_right)):
        for n, m in enumerate([(a, v) for a in (-1, 0, 1) for v in (0, b)]):
            ref[n] = values[m]


def third_kernel(colour, early, second, *refs):
    for old, mine in ((early, colour[0] < 2), (second, colour[0] == 2)):

        @pl.when(mine)
        def _(old=old):
            values = {m: old[idx(*m)] for m in OFFS}
            for m in OFFS:
                refs[-3][idx(*m)] = values[m]
            side_blocks(values, *refs[-2:])

    @pl.when(colour[0] == 3)
    def _():
        third_work(*refs)


def third_work(h_ref, from_left, from_right, interp, f_ref, to_left, to_right):
    rows = {(m, 0): h_ref[idx(*m)] for m in OFFS}
    rows[OWN, 1] = h_ref[9]
    own_interp = split(interp[...])
    for b, ref in ((-1, from_left), (1, from_right)):
        f = Factor()
        for n, key in enumerate(
            [((a, v), 0) for a in (-1, 0, 1) for v in (b, 0)] + [(OWN, 1)]
        ):
            f[key] = ref[n]
        subtract_fill(rows, f, OWN, own_interp, f.keys())
    result = solve([rows], [OWN], [own_interp])[0]
    values = {m: result[m, 0] for m in OFFS}
    for m in OFFS:
        f_ref[idx(*m)] = values[m]
    side_blocks(values, to_left, to_right)


def sums_kernel(f_ref, from_left, from_right, t_ref, up_ref, down_ref):
    f = {OWN: {m: split(f_ref[idx(*m)]) for m in OFFS}}
    for b, ref in ((-1, from_left), (1, from_right)):
        f[0, b] = {
            m: split(ref[n]) for n, m in enumerate([(a, v) for a in (-1, 0, 1) for v in (b, 0)])
        }
    turned = {
        (e, a): tuple(x.T for x in split_f32(f_ref, from_left, from_right, e, a))
        for e in f
        for a in (-1, 0, 1)
    }
    for a, ref in ((-1, up_ref), (0, t_ref), (1, down_ref)):
        across = [m for m in OFFS if a == 0 or m[0] in (0, a)]
        for n, m in enumerate(across):
            total = None
            for e in f:
                if m in f[e]:
                    term = dot_pair(split(turned[e, a][0]), f[e][m])
                    total = term if total is None else total + term
            ref[n] = total


def split_f32(f_ref, from_left, from_right, e, a):
    if e == OWN:
        return (f_ref[idx(a, 0)],)
    ref = from_left if e[1] < 0 else from_right
    return (ref[2 * (a + 1) + 1],)


def turned_pieces(total, below, above, details, wanted):
    mine = {}
    for n in wanted:
        value = total[n]
        if n >= 3:
            value = value + below[n - 3]
        if n < 6:
            value = value + above[n]
        value = -value
        if n == 4:
            value = value + jnp.where(eye(BLK), details[4:5, :], 0.0)
        mine[n] = value.T
    return mine


def gather(piece, start, tiles, per, at, width):
    return [
        piece[start + t * per : start + (t + 1) * per, at : at + width] for t in range(tiles)
    ]


def pack_lead(lead_per, per, total, below, above, details, lead_ref):
    mine = turned_pieces(total, below, above, details, HALF)
    for s, n in enumerate(HALF):
        piece = gather(mine[n], 0, lead_per // per, per, 0, lead_per)
        piece = jnp.concatenate(piece, axis=1) * (0.5 if n == 4 else 1.0)
        for d in range(lead_ref.shape[0]):
            lead_ref[d, s * per : (s + 1) * per, :] = piece


def pack_rest(lead_per, row_per, col_per, per, place, total, below, above, details, x_ref, yo_ref):
    mine = turned_pieces(total, below, above, details, ALL)
    tiles = lead_per // per
    grid_rows, grid_cols = yo_ref.shape[:2]
    for n in range(9):
        at = slice(n * per, (n + 1) * per)
        for_col = [gather(mine[n], 0, tiles, per, q * col_per, col_per) for q in range(grid_cols)]
        for r in range(grid_rows):
            d = lax.rem(r - place[2] + grid_rows, grid_rows)
            for_row = gather(mine[n], 0, tiles, per, r * row_per, row_per)
            x_ref[d, at, :] = jnp.concatenate(for_row, axis=1)
            for q in range(grid_cols):
                for_tile = gather(
                    mine[n], q * col_per, col_per // per, per, r * row_per, row_per
                )
                yo_ref[r, q, at, :] = jnp.concatenate(for_col[q] + for_tile, axis=1)


HALF = (4, 5, 6, 7, 8)
ALL = tuple(range(9))


def assemble(source, offsets, boxes, per, height, tiles, out_ref, base, grid_cols, near):
    depth = len(offsets) * per
    r = lax.broadcasted_iota(jnp.int32, (depth, TILE), 0)
    c = lax.broadcasted_iota(jnp.int32, (depth, TILE), 1)
    n, inner = r // per + offsets[0], r % per
    box = c % boxes
    same = inner == c // boxes
    box_row, box_col = box // grid_cols - (n // 3 - 1), box % grid_cols - (n % 3 - 1)

    def group(g, carry):
        values = []
        for s in range(8):
            b = g * 8 + s
            hot = same & (box_row == b // grid_cols) & (box_col == b % grid_cols)
            hot = hot.astype(f32).astype(bf16)
            hi, lo = split(source(b))
            values.append(dot(hi, hot) + dot(lo, hot))
        for t in range(tiles):
            part = jnp.stack([v[t * height : (t + 1) * height] for v in values], axis=0)
            part = jnp.swapaxes(part, 0, 1)
            across = slice(t * TILE, (t + 1) * TILE)
            for k in range(height):
                at = pl.ds(pl.multiple_of(base + k * boxes + g * 8, 8), 8)
                out_ref[at, across] = part[k] if near is None else part[k] + near[at, across]
        return carry

    lax.fori_loop(0, boxes // 8, group, 0)


def near_fill(row_ref, col_ref, out_ref, upper):
    def body(i, carry):
        at = pl.ds(pl.multiple_of(i * BLK, BLK), BLK)
        cx = column_of(row_ref[0:1, at] * scale)
        cy = column_of(row_ref[1:2, at] * scale)
        for j in range(out_ref.shape[1] // BLK):
            there = slice(j * BLK, (j + 1) * BLK)

            def work(there=there):
                out_ref[at, there] = kap(
                    cx, cy, col_ref[0:1, there] * scale, col_ref[1:2, there] * scale
                )

            if upper:
                pl.when(j >= i)(work)
            else:
                work()
        return carry

    lax.fori_loop(0, out_ref.shape[0] // BLK, body, 0)


def near_first(lead_pts, row_pts, col_pts, lead_ref, own_ref):
    near_fill(lead_pts, lead_pts, lead_ref, True)
    near_fill(row_pts, col_pts, own_ref, False)


def near_second(xy_pts, lead_pts, xy_ref):
    near_fill(xy_pts, lead_pts, xy_ref, False)


def lead_first(grid_cols, pack_ref, near, uh_ref, ul_ref, ih_ref, il_ref, rest_ref, mat, half):
    size = mat.shape[0]
    boxes = pack_ref.shape[0]
    per = TILE // boxes
    assemble(
        lambda b: pack_ref[b].T,
        HALF,
        boxes,
        per,
        size // boxes,
        size // TILE,
        half,
        0,
        grid_cols,
        None,
    )
    for i in range(size // BLK):
        here = slice(i * BLK, (i + 1) * BLK)
        for j in range(i, size // BLK):
            there = slice(j * BLK, (j + 1) * BLK)
            mat[here, there] = half[here, there] + half[there, here].T + near[here, there]
    lead_steps(mat, uh_ref, ul_ref, ih_ref, il_ref)
    done = uh_ref.shape[0]
    rest_ref[...] = mat[done:, done:]


def lead_second(rest_ref, uh_ref, ul_ref, ih_ref, il_ref, mat):
    mat[...] = rest_ref[...]
    lead_steps(mat, uh_ref, ul_ref, ih_ref, il_ref)


def lead_steps(mat, uh_ref, ul_ref, ih_ref, il_ref):
    pair = 2 * BLK
    size = mat.shape[0]
    for p in range(uh_ref.shape[0] // pair):
        start = p * pair
        a, b = slice(start, start + BLK), slice(start + BLK, start + pair)
        both, tail = slice(start, start + pair), slice(start + BLK, size)
        inv_a = factor([mat[a, a]])[0]
        split_a = split(inv_a)
        upper_a = dot_pair(split_a, split(mat[a, tail]))
        turned = split(upper_a[:, :BLK].T)
        lower = mat[b, tail] - dot_pair(turned, split(upper_a))
        inv_b = factor([lower[:, :BLK]])[0]
        split_b = split(inv_b)
        if start + pair < size:
            row = jnp.concatenate(
                [upper_a[:, BLK:], dot_pair(split_b, split(lower[:, BLK:]))], axis=0
            )
            hi, lo = split(row)
            uh_ref[both, start + pair :] = hi
            ul_ref[both, start + pair :] = lo
            for j in range(start + pair, size, pair):
                at = j - start - pair
                left = split(row[:, at : at + pair].T)
                rows = slice(j, j + pair)
                mat[rows, j:] = mat[rows, j:] - dot_pair(left, (hi[:, at:], lo[:, at:]))
        corner = -dot_pair(split_b, split(dot_pair(turned, split_a)))
        inv = jnp.concatenate(
            [
                jnp.concatenate([inv_a, jnp.zeros((BLK, BLK), f32)], axis=1),
                jnp.concatenate([corner, inv_b], axis=1),
            ],
            axis=0,
        )
        ih_ref[both, :], il_ref[both, :] = split(inv.T)


def tile_kernel(
    grid_cols,
    place,
    x_half,
    x_other,
    rest,
    near_xy,
    near_own,
    uh_first,
    ul_first,
    uh_second,
    ul_second,
    ih_first,
    il_first,
    ih_second,
    il_second,
    out_ref,
    mat,
    ph,
    plo,
    sems,
):
    total, size = mat.shape
    rows, cols = out_ref.shape
    boxes = rest.shape[0]
    per = TILE // boxes
    tiles = size // TILE
    row_per, col_per = rows // boxes, cols // boxes
    ends = [0, tiles * col_per]
    ends.append(ends[1] + cols // TILE * row_per)

    def part(n):
        return lambda b: rest[b].T[ends[n] : ends[n + 1]]

    def from_row(b):
        grid_rows = x_half.shape[1]
        d = lax.rem(place[2] - b // grid_cols + grid_rows, grid_rows)
        side = lax.bitwise_xor(place[3], b % grid_cols)
        k = side // 2
        odd = jnp.full((1, 1), side % 2, jnp.int32) == 1
        return jnp.where(odd, x_other[k, d], x_half[k, d]).T

    copies = [
        pltpu.make_async_copy(near_xy.at[:rows], mat.at[:rows], sems.at[0]),
        pltpu.make_async_copy(near_xy.at[rows:], mat.at[rows:], sems.at[1]),
        pltpu.make_async_copy(near_own, out_ref, sems.at[2]),
    ]
    for copy in copies:
        copy.start()
    copies[0].wait()
    assemble(from_row, ALL, boxes, per, row_per, tiles, mat, 0, grid_cols, mat)
    copies[1].wait()
    assemble(part(0), ALL, boxes, per, col_per, tiles, mat, rows, grid_cols, mat)
    pair = 2 * BLK
    chunk = 4 * BLK
    middle = uh_first.shape[0]

    def solve_rows(c, carry):
        at = pl.ds(pl.multiple_of(c * chunk, chunk), chunk)
        for p in range(size // pair):
            here = slice(p * pair, (p + 1) * pair)
            acc = mat[at, here]
            edge = min(p * pair, middle)
            if p > 0:
                acc = acc - dot_pair(
                    (ph[at, :edge], plo[at, :edge]), (uh_first[:edge, here], ul_first[:edge, here])
                )
            if p * pair > middle:
                before, above = slice(middle, p * pair), slice(0, p * pair - middle)
                across = slice(p * pair - middle, (p + 1) * pair - middle)
                acc = acc - dot_pair(
                    (ph[at, before], plo[at, before]),
                    (uh_second[above, across], ul_second[above, across]),
                )
            if p * pair < middle:
                inv = ih_first[here, :], il_first[here, :]
            else:
                across = slice(p * pair - middle, (p + 1) * pair - middle)
                inv = ih_second[across, :], il_second[across, :]
            value = dot_pair(split(acc), inv)
            mat[at, here] = value
            hi, lo = split(value)
            ph[at, here] = hi
            plo[at, here] = lo
        return carry

    lax.fori_loop(0, total // chunk, solve_rows, 0)
    copies[2].wait()
    first_row, first_col = place[0], place[1]

    @pl.when(first_col < size)
    def _():
        r = first_row + lax.broadcasted_iota(jnp.int32, (rows, cols), 0)
        c = first_col + lax.broadcasted_iota(jnp.int32, (rows, cols), 1)
        start = pl.multiple_of(first_col, BLK)
        out_ref[...] = jnp.where(r >= c, mat[:rows, pl.ds(start, cols)], 0.0)

    @pl.when(first_col >= size)
    def _():
        assemble(
            part(1), ALL, boxes, per, row_per, cols // TILE, out_ref, 0, grid_cols, out_ref
        )

        def update(c, carry):
            at = pl.ds(pl.multiple_of(c * chunk, chunk), chunk)
            value = out_ref[at, :] - dot_pair(
                (ph[at, :], plo[at, :]), (ph[rows:, :], plo[rows:, :]), nt=True
            )
            r = first_row + c * chunk + lax.broadcasted_iota(jnp.int32, (chunk, cols), 0)
            out_ref[at, :] = jnp.where(r >= size, value, 0.0)
            return carry

        lax.fori_loop(0, rows // chunk, update, 0)


def blocks(*counts):
    return [jax.ShapeDtypeStruct((n, BLK, BLK), f32) for n in counts]


def on_device(offsets, point_order, nugget, interp):
    row_at = lax.axis_index("row")
    col_at = lax.axis_index("col")
    row_count = lax.axis_size("row")
    col_count = lax.axis_size("col")
    box_total = row_count * col_count
    skel = interp.shape[2]
    box_id = row_at * col_count + col_at
    both = ("row", "col")

    corner = jnp.stack([row_at, col_at]).astype(f32)
    vmem = pl.BlockSpec(memory_space=pltpu.VMEM)
    smem = pl.BlockSpec(memory_space=pltpu.SMEM)
    packed = pl.pallas_call(
        order_kernel,
        in_specs=[smem] + [vmem] * 4,
        out_shape=jax.ShapeDtypeStruct((skel + 8, skel), f32),
        compiler_params=VMEM,
        name="order",
    )(corner, offsets[0, 0], point_order[0], nugget[0], interp[0, 0])
    details = packed[skel:]

    def exchange(x):
        return lax.all_to_all(x, both, split_axis=0, concat_axis=0, tiled=True)

    def hop(x, axis, distance):
        count = lax.axis_size(axis)
        return lax.ppermute(
            x, axis, [(i, i + distance) for i in range(count) if 0 <= i + distance < count]
        )

    def side_hop(x, distance, row_odd, col_odd):
        pairs = [
            (i * col_count + j, i * col_count + j + distance)
            for i in range(row_count)
            for j in range(col_count)
            if i % 2 == row_odd and j % 2 == col_odd and 0 <= j + distance < col_count
        ]
        return lax.ppermute(x, both, pairs)

    mid = jnp.stack([hop(packed, "row", 1), packed, hop(packed, "row", -1)])
    left = hop(mid, "col", 1)
    right = hop(mid, "col", -1)
    colour = 2 * (row_at % 2) + col_at % 2

    flag = colour[None].astype(jnp.int32)
    own_interp = interp[0, 0]

    def local(kernel, counts, name, *args):
        return pl.pallas_call(
            kernel,
            in_specs=[smem] + [vmem] * len(args),
            out_shape=blocks(*counts),
            compiler_params=VMEM,
            name=name,
        )(flag, *args)

    rows_3, pay_left, pay_right = local(rows_kernel_3, (10, 8, 8), "rows_3", mid, left, right)
    from_right = side_hop(pay_left, -1, 1, 1)
    from_left = side_hop(pay_right, 1, 1, 1)
    mid, left, right, rows_3 = lax.optimization_barrier((mid, left, right, rows_3))
    (rows_2,) = local(rows_kernel_2, (12,), "rows_2", mid, left, right)
    mid, left, right, rows_2, details = lax.optimization_barrier(
        (mid, left, right, rows_2, details)
    )
    everyone = exchange(jnp.broadcast_to(details[None], (box_total,) + details.shape))
    (early,) = local(early_kernel, (9,), "early", mid, left, right)
    second, pay_left, pay_right = local(
        second_kernel, (9, 7, 7), "second", rows_2, from_left, from_right, own_interp
    )
    from_right = side_hop(pay_left, -1, 1, 0)
    from_left = side_hop(pay_right, 1, 1, 0)
    f_own, pay_left, pay_right = local(
        third_kernel,
        (9, 6, 6),
        "third",
        early,
        second,
        rows_3,
        from_left,
        from_right,
        own_interp,
    )
    from_right = hop(pay_left, "col", -1)
    from_left = hop(pay_right, "col", 1)
    total, up, down = pl.pallas_call(
        sums_kernel, out_shape=blocks(9, 6, 6), compiler_params=VMEM, name="sums"
    )(f_own, from_left, from_right)
    from_below = hop(up, "row", -1)
    from_above = hop(down, "row", 1)
    lead = PANELS * PW
    lead_per = lead // box_total
    row_per = skel // row_count
    col_per = skel // col_count
    per = TILE // box_total
    lead_tiles = lead_per // per
    lanes = lead_tiles * col_per + col_per // per * row_per
    points = jnp.transpose(everyone[:, 0:3:2], (1, 2, 0))

    def flat(x):
        return jnp.pad(x.reshape(2, -1), ((0, 6), (0, 0)))

    lead_pts = flat(points[:, :lead_per])
    row_pts = lax.dynamic_slice_in_dim(points, row_at * row_per, row_per, 1)
    col_pts = lax.dynamic_slice_in_dim(points, col_at * col_per, col_per, 1)
    xy_pts = flat(jnp.concatenate([row_pts, col_pts], axis=1))
    row_pts, col_pts = flat(row_pts), flat(col_pts)
    rows_here = row_per * box_total
    cols_here = col_per * box_total
    both_rows = rows_here + cols_here
    total, lead_pts, xy_pts, row_pts, col_pts = lax.optimization_barrier(
        (total, lead_pts, xy_pts, row_pts, col_pts)
    )

    def near(kernel, shapes, name, *args):
        size = sum(r * c for r, c in shapes)
        return pl.pallas_call(
            kernel,
            out_shape=[jax.ShapeDtypeStruct(shape, f32) for shape in shapes],
            compiler_params=VMEM,
            cost_estimate=pl.CostEstimate(
                flops=20 * size, bytes_accessed=4 * size, transcendentals=2 * size
            ),
            name=name,
        )(*args)

    near_lead, near_own = near(
        near_first, [(lead, lead), (rows_here, cols_here)], "near_first", lead_pts, row_pts, col_pts
    )
    from_below, from_above, near_lead, near_own = lax.optimization_barrier(
        (from_below, from_above, near_lead, near_own)
    )
    sums = total, from_below, from_above, details
    lead_piece = pl.pallas_call(
        functools.partial(pack_lead, lead_per, per),
        out_shape=jax.ShapeDtypeStruct(
            (box_total, len(HALF) * per, lead_tiles * lead_per), f32
        ),
        compiler_params=VMEM,
        name="pack_lead",
    )(*sums)
    lead_pack = exchange(lead_piece)
    lead_piece, sums, *pts = lax.optimization_barrier((lead_piece, sums, xy_pts, lead_pts))
    place = jnp.stack([row_at * rows_here, col_at * cols_here, row_at, col_at]).astype(jnp.int32)
    for_rows, rest = pl.pallas_call(
        functools.partial(pack_rest, lead_per, row_per, col_per, per),
        in_specs=[smem] + [vmem] * 4,
        out_shape=[
            jax.ShapeDtypeStruct((row_count, 9 * per, lead_tiles * row_per), f32),
            jax.ShapeDtypeStruct((row_count, col_count, 9 * per, lanes), f32),
        ],
        compiler_params=VMEM,
        name="pack_rest",
    )(place, *sums)
    x_rows = jnp.stack(
        [for_rows[0]]
        + [
            lax.ppermute(for_rows[d], "row", [(i, (i + d) % row_count) for i in range(row_count)])
            for d in range(1, row_count)
        ]
    )
    (near_xy,) = near(near_second, [(both_rows, lead)], "near_second", *pts)
    rest, lead_pack, near_lead, near_xy, x_rows = lax.optimization_barrier(
        (rest, lead_pack, near_lead, near_xy, x_rows)
    )
    rest = exchange(rest.reshape(box_total, 9 * per, lanes))

    def swap(x, d):
        return lax.ppermute(x, "col", [(j, j ^ d) for j in range(col_count)])

    x_sides = [swap(x_rows, d) for d in range(2, col_count, 2)]
    middle = lead // 2

    def halves(rows, cols):
        return [jax.ShapeDtypeStruct((rows, cols), bf16)] * 2

    *first, remaining = pl.pallas_call(
        functools.partial(lead_first, col_count),
        out_shape=halves(middle, lead)
        + halves(middle, 2 * BLK)
        + [jax.ShapeDtypeStruct((lead - middle, lead - middle), f32)],
        scratch_shapes=[pltpu.VMEM((lead, lead), f32)] * 2,
        compiler_params=VMEM,
        name="lead_first",
    )(lead_pack, near_lead)
    remaining, x_sides, x_rows = lax.optimization_barrier((remaining, x_sides, x_rows))
    x_half = jnp.stack([x_rows] + x_sides)
    x_other = swap(x_half, 1)
    second = pl.pallas_call(
        lead_second,
        out_shape=halves(lead - middle, lead - middle) + halves(lead - middle, 2 * BLK),
        scratch_shapes=[pltpu.VMEM((lead - middle, lead - middle), f32)],
        compiler_params=VMEM,
        name="lead_second",
    )(remaining)
    return pl.pallas_call(
        functools.partial(tile_kernel, col_count),
        in_specs=[smem] + [vmem] * 3 + [pl.BlockSpec(memory_space=pl.ANY)] * 2 + [vmem] * 8,
        out_specs=vmem,
        out_shape=jax.ShapeDtypeStruct((rows_here, cols_here), f32),
        scratch_shapes=[
            pltpu.VMEM((both_rows, lead), f32),
            pltpu.VMEM((both_rows, lead), bf16),
            pltpu.VMEM((both_rows, lead), bf16),
            pltpu.SemaphoreType.DMA((3,)),
        ],
        compiler_params=VMEM,
        name="tile",
    )(
        place,
        x_half,
        x_other,
        rest,
        near_xy,
        near_own,
        *first[:2],
        *second[:2],
        *first[2:],
        *second[2:],
    )


def solution(mesh):
    in_specs = (
        P("row", "col", None, None),
        P("row", "col", None),
        P("row", "col", None),
        P("row", "col", None, None),
    )
    return jax.shard_map(
        on_device, mesh=mesh, in_specs=in_specs, out_specs=P("row", "col"), check_vma=False
    )
```

```python
import functools
import math

import jax
import jax.numpy as jnp
from jax import lax
from jax.experimental import pallas as pl
from jax.experimental.pallas import tpu as pltpu
from jax.sharding import PartitionSpec as P

PW = 512
PANELS = 2
kernel_amp = 0.015625
kernel_len = 0.5
scale = math.log2(math.e) / kernel_len
log_amp = math.log2(kernel_amp)
f32 = jnp.float32
bf16 = jnp.bfloat16
BLK = 128
TILE = 256
VMEM = pltpu.CompilerParams(vmem_limit_bytes=56 * 1024 * 1024)
OFFS = [(a, b) for a in (-1, 0, 1) for b in (-1, 0, 1)]


def idx(a, b):
    return (a + 1) * 3 + (b + 1)


def split(x):
    hi = x.astype(bf16)
    return hi, (x - hi.astype(f32)).astype(bf16)


def dot(a, b, nt=False):
    dims = ((1,), (1,)) if nt else ((1,), (0,))
    return lax.dot_general(a, b, (dims, ((), ())), preferred_element_type=f32)


def dot_pair(a, b, nt=False):
    left = jnp.concatenate([a[0], a[1], a[0]], axis=1)
    return dot(left, jnp.concatenate([b[0], b[0], b[1]], axis=1 if nt else 0), nt)


def dot3(a, b):
    return dot_pair(split(a), split(b))


def kap(cx, cy, rx, ry):
    dx = cx - rx
    dy = cy - ry
    d2 = dx * dx + dy * dy
    dist = d2 * lax.rsqrt(jnp.maximum(d2, 1e-30))
    return jnp.exp2(log_amp - dist)


def column_of(row):
    return jnp.broadcast_to(row, (BLK, BLK)).T


def eye(n):
    return lax.broadcasted_iota(jnp.int32, (n, n), 0) == lax.broadcasted_iota(
        jnp.int32, (n, n), 1
    )


def factor(mats, beside=()):
    n = mats[0].shape[0]
    w, part = (32, 16) if len(mats) == 1 else (16, 8)
    steps = -(-len(beside) * w // n)
    groups = range(w // 8)
    many = range(len(mats))
    cur = list(mats)
    out = [[] for _ in mats]
    lane = lax.broadcasted_iota(jnp.int32, (8, n), 1)
    sub = lax.broadcasted_iota(jnp.int32, (8, n), 0)
    for p in range(n // w):
        lo = p * w
        rows = [[c[8 * g : 8 * g + 8] for g in groups] for c in cur]
        unit = [[(lane == sub + (lo + 8 * g)).astype(f32) for g in groups] for _ in mats]
        upper = [[] for _ in mats]
        inner = [[] for _ in mats]
        for k in range(0, w, part):
            col = [
                [
                    [jnp.broadcast_to(f[g][:, lo + t : lo + t + 1], (8, n)) for g in groups]
                    for t in range(k, k + part)
                ]
                for f in rows
            ]
            for t in range(k, k + part):
                tg, tr = t // 8, t % 8
                below = range((t + 1) // 8, w // 8)
                for q in many:
                    c = col[q][t - k]
                    r = lax.rsqrt(c[tg][tr : tr + 1])
                    rp = r * r
                    row = rows[q][tg][tr : tr + 1]
                    one = unit[q][tg][tr : tr + 1]
                    upper[q].append(row * r)
                    inner[q].append(one * r)
                    for v in range(t + 1, k + part):
                        e = c[v // 8][v % 8 : v % 8 + 1]
                        for g in below:
                            if 8 * g + 7 >= v:
                                col[q][v - k][g] = col[q][v - k][g] - (c[g] * e) * rp
                    row, one = row * rp, one * rp
                    for g in below:
                        rows[q][g] = rows[q][g] - c[g] * row
                        unit[q][g] = unit[q][g] - c[g] * one
        at = lane[:1]
        inside = (at >= lo) & (at < lo + w)
        for q in many:
            u = jnp.concatenate(upper[q], axis=0)
            y = jnp.where(inside, jnp.concatenate(inner[q], axis=0), u)
            out[q].append(jnp.where(at < lo + w, y, 0.0))
            if lo + w < n:
                uh, ul = split(u)
                yh, yl = split(y)
                term = lax.dot_general(
                    jnp.concatenate([uh, ul, uh], axis=0),
                    jnp.concatenate([yh, yh, yl], axis=0),
                    (((0,), (0,)), ((), ())),
                    preferred_element_type=f32,
                )
                cur[q] = jnp.where(inside, 0.0, cur[q][w:]) - term[lo + w :]
        for _ in range(steps):
            if beside:
                beside.pop(0)()
    return [jnp.concatenate(o, axis=0) for o in out]


def order_kernel(corner, offsets, order, nugget, interp, out_ref):
    points = order.shape[1]
    table = jnp.concatenate(
        [
            offsets[0:1, :] + corner[0],
            offsets[1:2, :] + corner[1],
            nugget[...],
            jnp.zeros((13, points), f32),
        ],
        axis=0,
    )
    hot = lax.broadcasted_iota(jnp.int32, (points, points), 0) == order[...]
    hot = hot.astype(f32).astype(bf16)
    high, rest = table.astype(bf16), table
    rest = table - high.astype(f32)
    mid, low = split(rest)
    found = (dot(high, hot) + dot(mid, hot)) + dot(low, hot)
    skel = interp.shape[0]
    out_ref[:skel, :] = interp[...]
    parts = [found[i : i + 1, k : k + skel] for i in range(3) for k in (0, skel)]
    parts += [jnp.ones((1, skel), f32), jnp.zeros((1, skel), f32)]
    out_ref[skel:, :] = jnp.concatenate(parts, axis=0)


class Boxes:
    def __init__(self, sides):
        self.sides = sides
        self.kept = {}

    def row(self, c, n):
        return self.sides[c[1]][c[0] + 1, BLK + n : BLK + n + 1, :]

    def once(self, key, make):
        if key not in self.kept:
            self.kept[key] = make()
        return self.kept[key]

    def interp(self, c):
        return self.once(("i", c), lambda: split(self.sides[c[1]][c[0] + 1, :BLK, :]))

    def interp_t(self, c):
        return self.once(("t", c), lambda: split(self.sides[c[1]][c[0] + 1, :BLK, :].T))

    def place(self, c, n):
        value = self.row(c, n) * scale
        if n < 2 and c != OWN:
            value = value + (1.0 - self.row(c, 6)) * (1e6 * (1 + idx(*c)))
        return value

    def col(self, c, n):
        return self.once(("c", c, n), lambda: column_of(self.place(c, n)))

    def kernel(self, c, part, m, part_m):
        value = kap(
            self.col(c, part), self.col(c, 2 + part), self.place(m, part_m), self.place(m, 2 + part_m)
        )
        if c == m and part == part_m:
            weight = self.row(c, 4 + part) + (1.0 - self.row(c, 6))
            value = value + jnp.where(eye(BLK), weight, 0.0)
        return value

    def rows_of(self, c, wanted):
        result = {}
        for work in self.rows_later(result, c, wanted):
            work()
        return result

    def rows_later(self, result, c, wanted):
        wanted = list(wanted)

        def work(pair):
            skel = jnp.concatenate([self.kernel(c, 0, m, p) for m, p in pair], axis=1)
            red = jnp.concatenate([self.kernel(c, 1, m, p) for m, p in pair], axis=1)
            value = red - dot_pair(self.interp_t(c), split(skel))
            for k, key in enumerate(pair):
                result[key] = value[:, k * BLK : (k + 1) * BLK]

        return [functools.partial(work, wanted[n : n + 2]) for n in range(0, len(wanted), 2)]


def reduced(pair, interp):
    return pair[1] - dot_pair(split(pair[0]), interp)


class Factor(dict):
    def __init__(self, *args):
        super().__init__(*args)
        self.kept = {}

    def halves(self, key):
        if key not in self.kept:
            self.kept[key] = split(self[key])
        return self.kept[key]


def subtract_fill(rows, factor_e, at, interp, keys):
    gain = factor_e[at, 1] - dot_pair(factor_e.halves((at, 0)), interp)
    gain = split(gain.T)
    keys = [k for k in keys if k in rows]
    for n in range(0, len(keys), 2):
        pair = keys[n : n + 2]
        parts = [factor_e.halves(k) for k in pair]
        both = [jnp.concatenate([p[i] for p in parts], axis=1) for i in range(2)]
        value = dot_pair(gain, both)
        for k, key in enumerate(pair):
            rows[key] = rows[key] - value[:, k * BLK : (k + 1) * BLK]


def solve(rows_list, centres, interps, beside=()):
    mats = [reduced((r[c, 0], r[c, 1]), i) for r, c, i in zip(rows_list, centres, interps)]
    inverses = [split(u) for u in factor(mats, list(beside))]
    results = []
    for rows, centre, inv in zip(rows_list, centres, inverses):
        keys = [k for k in rows if k != (centre, 1)]
        result = Factor()
        for n in range(0, len(keys), 2):
            pair = keys[n : n + 2]
            value = dot_pair(inv, split(jnp.concatenate([rows[k] for k in pair], axis=1)))
            for k, key in enumerate(pair):
                result[key] = value[:, k * BLK : (k + 1) * BLK]
        results.append(result)
    return results


OWN = (0, 0)
ALL_SKEL = [(m, 0) for m in OFFS]


def own_solution(boxes, rows):
    return solve([rows], [OWN], [boxes.interp(OWN)])[0]


def colour_0(boxes):
    return own_solution(boxes, boxes.rows_of(OWN, ALL_SKEL + [(OWN, 1)]))


def colour_1(boxes):
    sources = [(0, b) for b in (-1, 1)]
    wanted = [
        [(OWN, 0), (OWN, 1), ((-1, 0), 0), ((1, 0), 0)]
        + [((a, b), 0) for a in (-1, 0, 1)]
        + [((0, b), 1)]
        for _, b in sources
    ]
    first = first_factors(boxes, sources, wanted)
    own = boxes.rows_of(OWN, ALL_SKEL + [(OWN, 1)])
    for f in first.values():
        subtract_fill(own, f, OWN, boxes.interp(OWN), f.keys())
    return own_solution(boxes, own)


def colour_2(boxes):
    sources = [(a, 0) for a in (-1, 1)]
    wanted = [
        [((0, b), p) for b in (-1, 0, 1) for p in (0, 1)]
        + [((a, b), 0) for b in (-1, 0, 1)]
        + [((a, 0), 1)]
        for a, _ in sources
    ]
    first = first_factors(boxes, sources, wanted)
    own = boxes.rows_of(OWN, ALL_SKEL + [((0, b), 1) for b in (-1, 0, 1)])
    for f in first.values():
        subtract_fill(own, f, OWN, boxes.interp(OWN), f.keys())
    return own


def colour_3(boxes):
    sources = [(a, b) for a in (-1, 1) for b in (-1, 1)]
    wanted = [
        [(m, p) for m in (OWN, (a, 0), (0, b), (a, b)) for p in (0, 1)] for a, b in sources
    ]
    second_at = [(-1, 0), (1, 0)]
    rows = [{} for _ in second_at]
    beside = []
    for (a, _), part in zip(second_at, rows):
        keys = [((a, 0), 0), ((a, 0), 1), (OWN, 0), (OWN, 1)]
        keys += [((0, b), p) for b in (-1, 1) for p in (0, 1)]
        keys += [((a, b), 0) for b in (-1, 1)]
        beside += boxes.rows_later(part, (a, 0), keys)
    first = first_factors(boxes, sources, wanted, beside)
    for (a, _), part in zip(second_at, rows):
        for b in (-1, 1):
            f = first[a, b]
            subtract_fill(part, f, (a, 0), boxes.interp((a, 0)), f.keys())
    own = {}
    beside = boxes.rows_later(own, OWN, ALL_SKEL + [(OWN, 1)])
    for f in first.values():
        beside.append(
            functools.partial(subtract_fill, own, f, OWN, boxes.interp(OWN), f.keys())
        )
    second = solve(rows, second_at, [boxes.interp(c) for c in second_at], beside)
    for f in second:
        subtract_fill(own, f, OWN, boxes.interp(OWN), f.keys())
    return own, second


def first_factors(boxes, sources, wanted, beside=()):
    found = solve(
        [boxes.rows_of(c, k) for c, k in zip(sources, wanted)],
        sources,
        [boxes.interp(c) for c in sources],
        beside,
    )
    return dict(zip(sources, found))


def early_kernel(colour, mid, left, right, f_ref):
    boxes = Boxes({0: mid, -1: left, 1: right})
    for mine, work in ((0, colour_0), (1, colour_1)):

        @pl.when(colour[0] == mine)
        def _(work=work):
            result = work(boxes)
            for m in OFFS:
                f_ref[idx(*m)] = result[m, 0]

        boxes.kept.clear()


def rows_kernel_2(colour, mid, left, right, h_ref):
    @pl.when(colour[0] == 2)
    def _():
        own = colour_2(Boxes({0: mid, -1: left, 1: right}))
        for key, value in own.items():
            h_ref[slot(key)] = value


def rows_kernel_3(colour, mid, left, right, h_ref, to_left, to_right):
    @pl.when(colour[0] == 3)
    def _():
        boxes = Boxes({0: mid, -1: left, 1: right})
        own, second = colour_3(boxes)
        for b, ref in ((-1, to_left), (1, to_right)):
            total = {}
            at = (0, b)
            order = [((a, v), 0) for a in (-1, 0, 1) for v in (b, 0)] + [(at, 1), (OWN, 1)]
            for key in order:
                total[key] = jnp.zeros((BLK, BLK), f32)
            for f in second:
                subtract_fill(total, f, at, boxes.interp(at), f.keys())
            for n, key in enumerate(order):
                ref[n] = -total[key]
        for key, value in own.items():
            h_ref[slot(key)] = value


def slot(key):
    return idx(*key[0]) if key[1] == 0 else red_slot(key[0][1])


def red_slot(b):
    return {0: 9, -1: 10, 1: 11}[b]


def second_kernel(colour, *refs):
    @pl.when(colour[0] == 2)
    def _():
        second_work(*refs)


def second_work(h_ref, from_left, from_right, interp, f_ref, to_left, to_right):
    rows = {(m, 0): h_ref[idx(*m)] for m in OFFS}
    for b in (-1, 0, 1):
        rows[(0, b), 1] = h_ref[red_slot(b)]
    for b, ref in ((-1, from_left), (1, from_right)):
        order = [((a, v), 0) for a in (-1, 0, 1) for v in (0, b)] + [(OWN, 1), ((0, b), 1)]
        for n, key in enumerate(order):
            rows[key] = rows[key] - ref[n]
    result = solve([rows], [OWN], [split(interp[...])])[0]
    for m in OFFS:
        f_ref[idx(*m)] = result[m, 0]
    for b, ref in ((-1, to_left), (1, to_right)):
        for n, key in enumerate(
            [((a, v), 0) for a in (-1, 0, 1) for v in (0, b)] + [((0, b), 1)]
        ):
            ref[n] = result[key]


def side_blocks(values, to_left, to_right):
    for b, ref in ((-1, to_left), (1, to_right)):
        for n, m in enumerate([(a, v) for a in (-1, 0, 1) for v in (0, b)]):
            ref[n] = values[m]


def third_kernel(colour, early, second, *refs):
    for old, mine in ((early, colour[0] < 2), (second, colour[0] == 2)):

        @pl.when(mine)
        def _(old=old):
            values = {m: old[idx(*m)] for m in OFFS}
            for m in OFFS:
                refs[-3][idx(*m)] = values[m]
            side_blocks(values, *refs[-2:])

    @pl.when(colour[0] == 3)
    def _():
        third_work(*refs)


def third_work(h_ref, from_left, from_right, interp, f_ref, to_left, to_right):
    rows = {(m, 0): h_ref[idx(*m)] for m in OFFS}
    rows[OWN, 1] = h_ref[9]
    own_interp = split(interp[...])
    for b, ref in ((-1, from_left), (1, from_right)):
        f = Factor()
        for n, key in enumerate(
            [((a, v), 0) for a in (-1, 0, 1) for v in (b, 0)] + [(OWN, 1)]
        ):
            f[key] = ref[n]
        subtract_fill(rows, f, OWN, own_interp, f.keys())
    result = solve([rows], [OWN], [own_interp])[0]
    values = {m: result[m, 0] for m in OFFS}
    for m in OFFS:
        f_ref[idx(*m)] = values[m]
    side_blocks(values, to_left, to_right)


def sums_kernel(f_ref, from_left, from_right, t_ref, up_ref, down_ref):
    f = {OWN: {m: split(f_ref[idx(*m)]) for m in OFFS}}
    for b, ref in ((-1, from_left), (1, from_right)):
        f[0, b] = {
            m: split(ref[n]) for n, m in enumerate([(a, v) for a in (-1, 0, 1) for v in (b, 0)])
        }
    turned = {
        (e, a): tuple(x.T for x in split_f32(f_ref, from_left, from_right, e, a))
        for e in f
        for a in (-1, 0, 1)
    }
    for a, ref in ((-1, up_ref), (0, t_ref), (1, down_ref)):
        across = [m for m in OFFS if a == 0 or m[0] in (0, a)]
        for n, m in enumerate(across):
            total = None
            for e in f:
                if m in f[e]:
                    term = dot_pair(split(turned[e, a][0]), f[e][m])
                    total = term if total is None else total + term
            ref[n] = total


def split_f32(f_ref, from_left, from_right, e, a):
    if e == OWN:
        return (f_ref[idx(a, 0)],)
    ref = from_left if e[1] < 0 else from_right
    return (ref[2 * (a + 1) + 1],)


def turned_pieces(total, below, above, details, wanted):
    mine = {}
    for n in wanted:
        value = total[n]
        if n >= 3:
            value = value + below[n - 3]
        if n < 6:
            value = value + above[n]
        value = -value
        if n == 4:
            value = value + jnp.where(eye(BLK), details[4:5, :], 0.0)
        mine[n] = value.T
    return mine


def gather(piece, start, tiles, per, at, width):
    return [
        piece[start + t * per : start + (t + 1) * per, at : at + width] for t in range(tiles)
    ]


def pack_lead(lead_per, per, total, below, above, details, lead_ref):
    mine = turned_pieces(total, below, above, details, HALF)
    for s, n in enumerate(HALF):
        piece = gather(mine[n], 0, lead_per // per, per, 0, lead_per)
        piece = jnp.concatenate(piece, axis=1) * (0.5 if n == 4 else 1.0)
        for d in range(lead_ref.shape[0]):
            lead_ref[d, s * per : (s + 1) * per, :] = piece


def pack_rest(lead_per, row_per, col_per, per, place, total, below, above, details, x_ref, yo_ref):
    mine = turned_pieces(total, below, above, details, ALL)
    tiles = lead_per // per
    grid_rows, grid_cols = yo_ref.shape[:2]
    for n in range(9):
        at = slice(n * per, (n + 1) * per)
        for_col = [gather(mine[n], 0, tiles, per, q * col_per, col_per) for q in range(grid_cols)]
        for r in range(grid_rows):
            d = lax.rem(r - place[2] + grid_rows, grid_rows)
            for_row = gather(mine[n], 0, tiles, per, r * row_per, row_per)
            x_ref[d, at, :] = jnp.concatenate(for_row, axis=1)
            for q in range(grid_cols):
                for_tile = gather(
                    mine[n], q * col_per, col_per // per, per, r * row_per, row_per
                )
                yo_ref[r, q, at, :] = jnp.concatenate(for_col[q] + for_tile, axis=1)


HALF = (4, 5, 6, 7, 8)
ALL = tuple(range(9))


def assemble(source, offsets, boxes, per, height, tiles, out_ref, base, grid_cols, near):
    depth = len(offsets) * per
    r = lax.broadcasted_iota(jnp.int32, (depth, TILE), 0)
    c = lax.broadcasted_iota(jnp.int32, (depth, TILE), 1)
    n, inner = r // per + offsets[0], r % per
    box = c % boxes
    same = inner == c // boxes
    box_row, box_col = box // grid_cols - (n // 3 - 1), box % grid_cols - (n % 3 - 1)

    def group(g, carry):
        values = []
        for s in range(8):
            b = g * 8 + s
            hot = same & (box_row == b // grid_cols) & (box_col == b % grid_cols)
            hot = hot.astype(f32).astype(bf16)
            hi, lo = split(source(b))
            values.append(dot(hi, hot) + dot(lo, hot))
        for t in range(tiles):
            part = jnp.stack([v[t * height : (t + 1) * height] for v in values], axis=0)
            part = jnp.swapaxes(part, 0, 1)
            across = slice(t * TILE, (t + 1) * TILE)
            for k in range(height):
                at = pl.ds(pl.multiple_of(base + k * boxes + g * 8, 8), 8)
                out_ref[at, across] = part[k] if near is None else part[k] + near[at, across]
        return carry

    lax.fori_loop(0, boxes // 8, group, 0)


def near_fill(row_ref, col_ref, out_ref, upper):
    def body(i, carry):
        at = pl.ds(pl.multiple_of(i * BLK, BLK), BLK)
        cx = column_of(row_ref[0:1, at] * scale)
        cy = column_of(row_ref[1:2, at] * scale)
        for j in range(out_ref.shape[1] // BLK):
            there = slice(j * BLK, (j + 1) * BLK)

            def work(there=there):
                out_ref[at, there] = kap(
                    cx, cy, col_ref[0:1, there] * scale, col_ref[1:2, there] * scale
                )

            if upper:
                pl.when(j >= i)(work)
            else:
                work()
        return carry

    lax.fori_loop(0, out_ref.shape[0] // BLK, body, 0)


def near_first(lead_pts, row_pts, col_pts, lead_ref, own_ref):
    near_fill(lead_pts, lead_pts, lead_ref, True)
    near_fill(row_pts, col_pts, own_ref, False)


def near_second(xy_pts, lead_pts, xy_ref):
    near_fill(xy_pts, lead_pts, xy_ref, False)


def lead_first(grid_cols, pack_ref, near, uh_ref, ul_ref, ih_ref, il_ref, rest_ref, mat, half):
    size = mat.shape[0]
    boxes = pack_ref.shape[0]
    per = TILE // boxes
    assemble(
        lambda b: pack_ref[b].T,
        HALF,
        boxes,
        per,
        size // boxes,
        size // TILE,
        half,
        0,
        grid_cols,
        None,
    )
    for i in range(size // BLK):
        here = slice(i * BLK, (i + 1) * BLK)
        for j in range(i, size // BLK):
            there = slice(j * BLK, (j + 1) * BLK)
            mat[here, there] = half[here, there] + half[there, here].T + near[here, there]
    lead_steps(mat, uh_ref, ul_ref, ih_ref, il_ref)
    done = uh_ref.shape[0]
    rest_ref[...] = mat[done:, done:]


def lead_second(rest_ref, uh_ref, ul_ref, ih_ref, il_ref, mat):
    mat[...] = rest_ref[...]
    lead_steps(mat, uh_ref, ul_ref, ih_ref, il_ref)


def lead_steps(mat, uh_ref, ul_ref, ih_ref, il_ref):
    pair = 2 * BLK
    size = mat.shape[0]
    for p in range(uh_ref.shape[0] // pair):
        start = p * pair
        a, b = slice(start, start + BLK), slice(start + BLK, start + pair)
        both, tail = slice(start, start + pair), slice(start + BLK, size)
        inv_a = factor([mat[a, a]])[0]
        split_a = split(inv_a)
        upper_a = dot_pair(split_a, split(mat[a, tail]))
        turned = split(upper_a[:, :BLK].T)
        lower = mat[b, tail] - dot_pair(turned, split(upper_a))
        inv_b = factor([lower[:, :BLK]])[0]
        split_b = split(inv_b)
        if start + pair < size:
            row = jnp.concatenate(
                [upper_a[:, BLK:], dot_pair(split_b, split(lower[:, BLK:]))], axis=0
            )
            hi, lo = split(row)
            uh_ref[both, start + pair :] = hi
            ul_ref[both, start + pair :] = lo
            for j in range(start + pair, size, pair):
                at = j - start - pair
                left = split(row[:, at : at + pair].T)
                rows = slice(j, j + pair)
                mat[rows, j:] = mat[rows, j:] - dot_pair(left, (hi[:, at:], lo[:, at:]))
        corner = -dot_pair(split_b, split(dot_pair(turned, split_a)))
        inv = jnp.concatenate(
            [
                jnp.concatenate([inv_a, jnp.zeros((BLK, BLK), f32)], axis=1),
                jnp.concatenate([corner, inv_b], axis=1),
            ],
            axis=0,
        )
        ih_ref[both, :], il_ref[both, :] = split(inv.T)


def tile_kernel(
    grid_cols,
    place,
    x_half,
    x_other,
    rest,
    near_xy,
    near_own,
    uh_first,
    ul_first,
    uh_second,
    ul_second,
    ih_first,
    il_first,
    ih_second,
    il_second,
    out_ref,
    mat,
    ph,
    plo,
    sems,
):
    total, size = mat.shape
    rows, cols = out_ref.shape
    boxes = rest.shape[0]
    per = TILE // boxes
    tiles = size // TILE
    row_per, col_per = rows // boxes, cols // boxes
    ends = [0, tiles * col_per]
    ends.append(ends[1] + cols // TILE * row_per)

    def part(n):
        return lambda b: rest[b].T[ends[n] : ends[n + 1]]

    def from_row(b):
        grid_rows = x_half.shape[1]
        d = lax.rem(place[2] - b // grid_cols + grid_rows, grid_rows)
        side = lax.bitwise_xor(place[3], b % grid_cols)
        k = side // 2
        odd = jnp.full((1, 1), side % 2, jnp.int32) == 1
        return jnp.where(odd, x_other[k, d], x_half[k, d]).T

    copies = [
        pltpu.make_async_copy(near_xy.at[:rows], mat.at[:rows], sems.at[0]),
        pltpu.make_async_copy(near_xy.at[rows:], mat.at[rows:], sems.at[1]),
        pltpu.make_async_copy(near_own, out_ref, sems.at[2]),
    ]
    for copy in copies:
        copy.start()
    copies[0].wait()
    assemble(from_row, ALL, boxes, per, row_per, tiles, mat, 0, grid_cols, mat)
    copies[1].wait()
    assemble(part(0), ALL, boxes, per, col_per, tiles, mat, rows, grid_cols, mat)
    pair = 2 * BLK
    chunk = 4 * BLK
    wide = 3 * chunk if total % (3 * chunk) == 0 else chunk
    middle = uh_first.shape[0]

    def solve_rows(c, carry):
        at = pl.ds(pl.multiple_of(c * wide, wide), wide)
        for p in range(size // pair):
            here = slice(p * pair, (p + 1) * pair)
            acc = mat[at, here]
            edge = min(p * pair, middle)
            if p > 0:
                acc = acc - dot_pair(
                    (ph[at, :edge], plo[at, :edge]), (uh_first[:edge, here], ul_first[:edge, here])
                )
            if p * pair > middle:
                before, above = slice(middle, p * pair), slice(0, p * pair - middle)
                across = slice(p * pair - middle, (p + 1) * pair - middle)
                acc = acc - dot_pair(
                    (ph[at, before], plo[at, before]),
                    (uh_second[above, across], ul_second[above, across]),
                )
            if p * pair < middle:
                inv = ih_first[here, :], il_first[here, :]
            else:
                across = slice(p * pair - middle, (p + 1) * pair - middle)
                inv = ih_second[across, :], il_second[across, :]
            value = dot_pair(split(acc), inv)
            mat[at, here] = value
            hi, lo = split(value)
            ph[at, here] = hi
            plo[at, here] = lo
        return carry

    lax.fori_loop(0, total // wide, solve_rows, 0)
    copies[2].wait()
    first_row, first_col = place[0], place[1]

    @pl.when(first_col < size)
    def _():
        r = first_row + lax.broadcasted_iota(jnp.int32, (rows, cols), 0)
        c = first_col + lax.broadcasted_iota(jnp.int32, (rows, cols), 1)
        start = pl.multiple_of(first_col, BLK)
        out_ref[...] = jnp.where(r >= c, mat[:rows, pl.ds(start, cols)], 0.0)

    @pl.when(first_col >= size)
    def _():
        assemble(
            part(1), ALL, boxes, per, row_per, cols // TILE, out_ref, 0, grid_cols, out_ref
        )

        def update(c, carry):
            at = pl.ds(pl.multiple_of(c * chunk, chunk), chunk)
            value = out_ref[at, :] - dot_pair(
                (ph[at, :], plo[at, :]), (ph[rows:, :], plo[rows:, :]), nt=True
            )
            r = first_row + c * chunk + lax.broadcasted_iota(jnp.int32, (chunk, cols), 0)
            out_ref[at, :] = jnp.where(r >= size, value, 0.0)
            return carry

        lax.fori_loop(0, rows // chunk, update, 0)


def blocks(*counts):
    return [jax.ShapeDtypeStruct((n, BLK, BLK), f32) for n in counts]


def on_device(offsets, point_order, nugget, interp):
    row_at = lax.axis_index("row")
    col_at = lax.axis_index("col")
    row_count = lax.axis_size("row")
    col_count = lax.axis_size("col")
    box_total = row_count * col_count
    skel = interp.shape[2]
    box_id = row_at * col_count + col_at
    both = ("row", "col")

    corner = jnp.stack([row_at, col_at]).astype(f32)
    vmem = pl.BlockSpec(memory_space=pltpu.VMEM)
    smem = pl.BlockSpec(memory_space=pltpu.SMEM)
    packed = pl.pallas_call(
        order_kernel,
        in_specs=[smem] + [vmem] * 4,
        out_shape=jax.ShapeDtypeStruct((skel + 8, skel), f32),
        compiler_params=VMEM,
        name="order",
    )(corner, offsets[0, 0], point_order[0], nugget[0], interp[0, 0])
    details = packed[skel:]

    def exchange(x):
        return lax.all_to_all(x, both, split_axis=0, concat_axis=0, tiled=True)

    def hop(x, axis, distance):
        count = lax.axis_size(axis)
        return lax.ppermute(
            x, axis, [(i, i + distance) for i in range(count) if 0 <= i + distance < count]
        )

    def side_hop(x, distance, row_odd, col_odd):
        pairs = [
            (i * col_count + j, i * col_count + j + distance)
            for i in range(row_count)
            for j in range(col_count)
            if i % 2 == row_odd and j % 2 == col_odd and 0 <= j + distance < col_count
        ]
        return lax.ppermute(x, both, pairs)

    mid = jnp.stack([hop(packed, "row", 1), packed, hop(packed, "row", -1)])
    left = hop(mid, "col", 1)
    right = hop(mid, "col", -1)
    colour = 2 * (row_at % 2) + col_at % 2

    flag = colour[None].astype(jnp.int32)
    own_interp = interp[0, 0]

    def local(kernel, counts, name, *args):
        return pl.pallas_call(
            kernel,
            in_specs=[smem] + [vmem] * len(args),
            out_shape=blocks(*counts),
            compiler_params=VMEM,
            name=name,
        )(flag, *args)

    rows_3, pay_left, pay_right = local(rows_kernel_3, (10, 8, 8), "rows_3", mid, left, right)
    from_right = side_hop(pay_left, -1, 1, 1)
    from_left = side_hop(pay_right, 1, 1, 1)
    mid, left, right, rows_3 = lax.optimization_barrier((mid, left, right, rows_3))
    (rows_2,) = local(rows_kernel_2, (12,), "rows_2", mid, left, right)
    mid, left, right, rows_2, details = lax.optimization_barrier(
        (mid, left, right, rows_2, details)
    )
    everyone = exchange(jnp.broadcast_to(details[None], (box_total,) + details.shape))
    (early,) = local(early_kernel, (9,), "early", mid, left, right)
    second, pay_left, pay_right = local(
        second_kernel, (9, 7, 7), "second", rows_2, from_left, from_right, own_interp
    )
    from_right = side_hop(pay_left, -1, 1, 0)
    from_left = side_hop(pay_right, 1, 1, 0)
    f_own, pay_left, pay_right = local(
        third_kernel,
        (9, 6, 6),
        "third",
        early,
        second,
        rows_3,
        from_left,
        from_right,
        own_interp,
    )
    from_right = hop(pay_left, "col", -1)
    from_left = hop(pay_right, "col", 1)
    total, up, down = pl.pallas_call(
        sums_kernel, out_shape=blocks(9, 6, 6), compiler_params=VMEM, name="sums"
    )(f_own, from_left, from_right)
    from_below = hop(up, "row", -1)
    from_above = hop(down, "row", 1)
    lead = PANELS * PW
    lead_per = lead // box_total
    row_per = skel // row_count
    col_per = skel // col_count
    per = TILE // box_total
    lead_tiles = lead_per // per
    lanes = lead_tiles * col_per + col_per // per * row_per
    points = jnp.transpose(everyone[:, 0:3:2], (1, 2, 0))

    def flat(x):
        return jnp.pad(x.reshape(2, -1), ((0, 6), (0, 0)))

    lead_pts = flat(points[:, :lead_per])
    row_pts = lax.dynamic_slice_in_dim(points, row_at * row_per, row_per, 1)
    col_pts = lax.dynamic_slice_in_dim(points, col_at * col_per, col_per, 1)
    xy_pts = flat(jnp.concatenate([row_pts, col_pts], axis=1))
    row_pts, col_pts = flat(row_pts), flat(col_pts)
    rows_here = row_per * box_total
    cols_here = col_per * box_total
    both_rows = rows_here + cols_here
    total, lead_pts, xy_pts, row_pts, col_pts = lax.optimization_barrier(
        (total, lead_pts, xy_pts, row_pts, col_pts)
    )

    def near(kernel, shapes, name, *args):
        size = sum(r * c for r, c in shapes)
        return pl.pallas_call(
            kernel,
            out_shape=[jax.ShapeDtypeStruct(shape, f32) for shape in shapes],
            compiler_params=VMEM,
            cost_estimate=pl.CostEstimate(
                flops=20 * size, bytes_accessed=4 * size, transcendentals=2 * size
            ),
            name=name,
        )(*args)

    near_lead, near_own = near(
        near_first, [(lead, lead), (rows_here, cols_here)], "near_first", lead_pts, row_pts, col_pts
    )
    from_below, from_above, near_lead, near_own = lax.optimization_barrier(
        (from_below, from_above, near_lead, near_own)
    )
    sums = total, from_below, from_above, details
    lead_piece = pl.pallas_call(
        functools.partial(pack_lead, lead_per, per),
        out_shape=jax.ShapeDtypeStruct(
            (box_total, len(HALF) * per, lead_tiles * lead_per), f32
        ),
        compiler_params=VMEM,
        name="pack_lead",
    )(*sums)
    lead_pack = exchange(lead_piece)
    lead_piece, sums, *pts = lax.optimization_barrier((lead_piece, sums, xy_pts, lead_pts))
    place = jnp.stack([row_at * rows_here, col_at * cols_here, row_at, col_at]).astype(jnp.int32)
    for_rows, rest = pl.pallas_call(
        functools.partial(pack_rest, lead_per, row_per, col_per, per),
        in_specs=[smem] + [vmem] * 4,
        out_shape=[
            jax.ShapeDtypeStruct((row_count, 9 * per, lead_tiles * row_per), f32),
            jax.ShapeDtypeStruct((row_count, col_count, 9 * per, lanes), f32),
        ],
        compiler_params=VMEM,
        name="pack_rest",
    )(place, *sums)
    x_rows = jnp.stack(
        [for_rows[0]]
        + [
            lax.ppermute(for_rows[d], "row", [(i, (i + d) % row_count) for i in range(row_count)])
            for d in range(1, row_count)
        ]
    )
    (near_xy,) = near(near_second, [(both_rows, lead)], "near_second", *pts)
    rest, lead_pack, near_lead, near_xy, x_rows = lax.optimization_barrier(
        (rest, lead_pack, near_lead, near_xy, x_rows)
    )
    rest = exchange(rest.reshape(box_total, 9 * per, lanes))

    def swap(x, d):
        return lax.ppermute(x, "col", [(j, j ^ d) for j in range(col_count)])

    x_sides = [swap(x_rows, d) for d in range(2, col_count, 2)]
    middle = lead // 2

    def halves(rows, cols):
        return [jax.ShapeDtypeStruct((rows, cols), bf16)] * 2

    *first, remaining = pl.pallas_call(
        functools.partial(lead_first, col_count),
        out_shape=halves(middle, lead)
        + halves(middle, 2 * BLK)
        + [jax.ShapeDtypeStruct((lead - middle, lead - middle), f32)],
        scratch_shapes=[pltpu.VMEM((lead, lead), f32)] * 2,
        compiler_params=VMEM,
        name="lead_first",
    )(lead_pack, near_lead)
    remaining, x_sides, x_rows = lax.optimization_barrier((remaining, x_sides, x_rows))
    x_half = jnp.stack([x_rows] + x_sides)
    x_other = swap(x_half, 1)
    second = pl.pallas_call(
        lead_second,
        out_shape=halves(lead - middle, lead - middle) + halves(lead - middle, 2 * BLK),
        scratch_shapes=[pltpu.VMEM((lead - middle, lead - middle), f32)],
        compiler_params=VMEM,
        name="lead_second",
    )(remaining)
    return pl.pallas_call(
        functools.partial(tile_kernel, col_count),
        in_specs=[smem] + [vmem] * 3 + [pl.BlockSpec(memory_space=pl.ANY)] * 2 + [vmem] * 8,
        out_specs=vmem,
        out_shape=jax.ShapeDtypeStruct((rows_here, cols_here), f32),
        scratch_shapes=[
            pltpu.VMEM((both_rows, lead), f32),
            pltpu.VMEM((both_rows, lead), bf16),
            pltpu.VMEM((both_rows, lead), bf16),
            pltpu.SemaphoreType.DMA((3,)),
        ],
        compiler_params=VMEM,
        name="tile",
    )(
        place,
        x_half,
        x_other,
        rest,
        near_xy,
        near_own,
        *first[:2],
        *second[:2],
        *first[2:],
        *second[2:],
    )


def solution(mesh):
    in_specs = (
        P("row", "col", None, None),
        P("row", "col", None),
        P("row", "col", None),
        P("row", "col", None, None),
    )
    return jax.shard_map(
        on_device, mesh=mesh, in_specs=in_specs, out_specs=P("row", "col"), check_vma=False
    )
```
